512 devices in a mesh: tx: 16 (over y, x_hi, core), mp: 16 (over z), rep: 2 (over x_lo).
Axes of the slice: x: 4 (x_hi: 2, x_lo: 2; x = x_hi * 2 + x_lo), y: 4, z: 16, core: 2. Of those that a mesh axis runs over, the one named last changes fastest.
Arguments:
- jacobian: bfloat16 [16, 8192, 2048], P('tx', ('mp', 'rep')), may hold values from -0.44921875 to 0.44921875
- coupling: float32 [4, 16, 8192], P(None, 'tx', ('mp', 'rep')), may hold values from 0.2 to 2
- brick_left: int32 [16, 32, 24], P('tx', ('mp', 'rep')), may hold values from 0 to 7
- brick_right: int32 [16, 32, 24], P('tx', ('mp', 'rep')), may hold values from 0 to 7
- tile_target: int32 [16, 32, 24], P('tx', ('mp', 'rep')), may hold values from 0 to 127, as said below
Outputs:
- normal_tiles: float32 [128, 256, 256], P('mp', ('tx', 'rep'))
The draws below stay inside these ranges and needn't reach their ends.
Inputs may be any that keep to these rules, and one draw needn't show every extreme that they name: Among the 24 entries of one row tile_target[t, b, :], no owner (entry // 8) occurs more than 2 times; in every row some owner occurs exactly 2 times, the same owner for all rows b of one t with the same remainder of b divided by the number of rep devices.
All inputs are finite; a program needn't handle non-finite values.
Results may differ from the reference program's by a relative error of at most 0.0039.
Values may be sent and summed in bfloat16 or wider, within the bound.
No kernel may reach another device: no remote copies, remote signals or barrier semaphores. Data moves between devices by JAX's collectives and lax.ppermute only.
A program may use at most 64 MiB of HBM per device.

```python
import math
import jax
import jax.numpy as jnp
from jax import lax

BRICK = 256
FOOT_BRICKS = 8
ROWS = 256
STEPS = 4
LISTED = 6
TILES_DEV = 8
FOOT = 2048
PAIRS = 24
TXS = 16
BLOCKS = 32
DATA = 8192
TILES = 128
CAP = 2


def draw_tile_target(key, part):
    key = jax.random.fold_in(key, 5)
    owners = TILES // TILES_DEV
    subsets = BLOCKS // owners
    hot_table = jax.random.randint(jax.random.fold_in(key, 1), (TXS, subsets), 0, owners)
    block_index = jnp.arange(BLOCKS) % subsets
    hot = hot_table[:, block_index].reshape(-1)
    keys = jax.random.split(jax.random.fold_in(key, 2), TXS * BLOCKS)

    def one_row(row_key, hot_owner):
        first_key, second_key, third_key = jax.random.split(row_key, 3)
        others = jax.random.permutation(first_key, (owners - 1) * CAP)[:PAIRS - CAP]
        other_owner = (hot_owner + 1 + others // CAP) % owners
        owner = jnp.concatenate([jnp.full((CAP,), hot_owner, jnp.int32), other_owner.astype(jnp.int32)])
        owner = owner[jax.random.permutation(second_key, PAIRS)]
        local = jax.random.randint(third_key, (PAIRS,), 0, TILES_DEV)
        return (owner * TILES_DEV + local).astype(jnp.int32)
    return jax.vmap(one_row)(keys, hot).reshape(TXS, BLOCKS, PAIRS).astype(jnp.int32)


def place_ends(entries, stream_key, least, high):
    place = [jax.random.randint(jax.random.fold_in(stream_key, axis), (), 0, length) for axis, length in enumerate(entries.shape)]
    longest = entries.shape.index(max(entries.shape))
    next_to = place[:longest] + [(place[longest] + 1) % entries.shape[longest]] + place[longest + 1:]
    return entries.at[tuple(place)].set(least).at[tuple(next_to)].set(high)


def levels(rng, shape, shards, least, top_value):
    gain = 1.0
    for position, shards_of in shards:
        heights = jax.random.uniform(jax.random.fold_in(jax.random.fold_in(rng, 6), position), (shards_of,), jnp.float32, least / len(shards), top_value / len(shards))
        gain = gain * jnp.repeat(jnp.exp(heights), shape[position] // shards_of).reshape((-1,) + (1,) * (len(shape) - 1 - position))
    return gain


def noise(rng, dims, spread, bound, pieces=(), dtype=jnp.bfloat16):
    result = jax.random.normal(rng, dims, jnp.float32) * spread
    if len(pieces) > 0:
        result = levels(rng, dims, pieces, -0.22, 0.18) * result
    return jnp.clip(result, min=-bound, max=bound).astype(dtype)


def setup_inputs(seed: int = 0) -> dict:
    seeds = jax.random.split(jax.random.key(seed), 6)
    jacobian = noise(seeds[0], (TXS, DATA, FOOT), 0.07, 0.44921875, ((0, 16), (1, 32)))
    coupling = jnp.clip(jnp.exp(math.log(2.0) - 2.3025851 * jax.random.uniform(seeds[1], (STEPS, TXS, DATA), jnp.float32) ** levels(seeds[1], (STEPS, TXS, DATA), ((1, 16), (2, 32)), -0.2, 0.2)), 0.2, 2.0)
    brick_left = place_ends(jax.random.randint(seeds[2], (TXS, BLOCKS, PAIRS), 0, FOOT_BRICKS), jax.random.fold_in(seeds[2], 1), 0, FOOT_BRICKS - 1).astype(jnp.int32)
    brick_right = place_ends(jax.random.randint(seeds[3], (TXS, BLOCKS, PAIRS), 0, FOOT_BRICKS), jax.random.fold_in(seeds[3], 1), 0, FOOT_BRICKS - 1).astype(jnp.int32)
    tile_target = draw_tile_target(jax.random.fold_in(seeds[5], 71), 0)
    return dict(jacobian=jacobian, coupling=coupling, brick_left=brick_left, brick_right=brick_right, tile_target=tile_target)


def reference(jacobian, coupling, brick_left, brick_right, tile_target):
    def one_block(index, total):
        t = (index // BLOCKS).astype(jnp.int32)
        b = (index % BLOCKS).astype(jnp.int32)
        start = (b * ROWS).astype(jnp.int32)
        zero = jnp.int32(0)
        own = lax.dynamic_slice(jacobian, (t, start, zero), (1, ROWS, FOOT))[0].reshape(ROWS, FOOT_BRICKS, BRICK)
        tiles = []
        for step in range(STEPS):
            partner = ((t + step) % TXS).astype(jnp.int32)
            other = lax.dynamic_slice(jacobian, (partner, start, zero), (1, ROWS, FOOT))[0].reshape(ROWS, FOOT_BRICKS, BRICK)
            weight = lax.dynamic_slice(coupling, (jnp.int32(step), t, start), (1, 1, ROWS))[0, 0]
            first = jnp.int32(step * LISTED)
            left_ids = lax.dynamic_slice(brick_left, (t, b, first), (1, 1, LISTED))[0, 0]
            right_ids = lax.dynamic_slice(brick_right, (t, b, first), (1, 1, LISTED))[0, 0]
            left = (jnp.take(own, left_ids, axis=1).astype(jnp.float32) * weight[:, None, None]).astype(jnp.bfloat16)
            right = jnp.take(other, right_ids, axis=1)
            part = jnp.einsum('rla,rlb->lab', left.astype(jnp.float32), right.astype(jnp.float32))
            rounded = lax.optimization_barrier(part.astype(jnp.bfloat16))
            tiles.append(rounded.astype(jnp.float32))
        targets = lax.dynamic_slice(tile_target, (t, b, zero), (1, 1, PAIRS))[0, 0]
        return total.at[targets].add(jnp.concatenate(tiles, axis=0))

    start_total = jnp.zeros((TILES, BRICK, BRICK), jnp.float32)
    return lax.fori_loop(0, TXS * BLOCKS, one_block, start_total)
```

```python
import jax
import jax.numpy as jnp
from jax import lax
from jax.experimental import pallas as pl
from jax.experimental.pallas import tpu as pltpu
from jax.sharding import PartitionSpec as P

BRICK = 256
STEPS = 4
LISTED = 6
PAIRS = STEPS * LISTED
TILES_DEV = 8
PLANE = ("tx", "rep")
HELD = ((0, 0), (0, 1), (1, 2), (0, 2))


def fetched(block, distance):
    devices = lax.axis_size("tx")
    route = [((i + distance) % devices, i) for i in range(devices)]
    return lax.ppermute(block, "tx", route)


def exchanged(block, axis):
    return lax.all_to_all(block, axis, split_axis=0, concat_axis=0, tiled=True)


def product_kernel(left_ids, right_ids, weight, own, second, fourth, out):
    blocks = (own, second, fourth)
    parts, rows, _ = out.shape
    slab = rows // PAIRS

    def brick(block, index):
        return block[:, pl.ds(pl.multiple_of(index * BRICK, BRICK), BRICK)]

    for first in range(0, PAIRS, 2):
        step = first // LISTED
        left_block, right_block = (blocks[i] for i in HELD[step])
        pair = []
        for entry in (first, first + 1):
            left = brick(left_block, left_ids[entry]).astype(jnp.float32) * weight[:, step : step + 1]
            tile = lax.dot_general(
                left.astype(jnp.bfloat16),
                brick(right_block, right_ids[entry]),
                (((0,), (0,)), ((), ())),
                preferred_element_type=jnp.float32,
            )
            pair.append(tile.reshape(parts, slab, BRICK))
        out[:, first * slab : (first + 2) * slab, :] = jnp.concatenate(pair, axis=1).astype(jnp.bfloat16)


def sum_kernel(labels, got, out, total):
    parts, rows, _ = got.shape
    slab = rows // PAIRS
    total[...] = jnp.zeros_like(total)

    def one_part(part, carry):
        for first in range(0, PAIRS, 2):
            both = got[part, first * slab : (first + 2) * slab, :].astype(jnp.float32)
            for half in range(2):
                tile = labels[part * PAIRS + first + half]
                total[tile] += both[half * slab : (half + 1) * slab]
        return carry

    lax.fori_loop(0, parts, one_part, 0)
    out[...] = total[...].reshape(out.shape).astype(out.dtype)


def body(jacobian, coupling, brick_left, brick_right, tile_target):
    own = jacobian[0]
    rows = own.shape[0]
    weight = coupling[:, 0]
    left_ids, right_ids = brick_left[0, 0], brick_right[0, 0]
    parts = lax.axis_size("tx") * lax.axis_size("rep")
    owners = lax.axis_size("mp")
    slab = BRICK // parts
    tiles = owners * TILES_DEV

    second = fetched(own, 1)
    fourth = fetched(own, 3)
    middle = slice(2 * LISTED, 3 * LISTED)
    small = jnp.concatenate(
        [weight[2], left_ids[middle].astype(jnp.float32), right_ids[middle].astype(jnp.float32)]
    )
    small = fetched(small, 1)
    weight = weight.at[2].set(small[:rows])
    left_ids = left_ids.at[middle].set(small[rows : rows + LISTED].astype(jnp.int32))
    right_ids = right_ids.at[middle].set(small[rows + LISTED :].astype(jnp.int32))

    labels = exchanged(jnp.broadcast_to(tile_target[0], (parts, PAIRS)), PLANE)
    labels = labels.reshape(lax.axis_size("tx"), lax.axis_size("rep"), STEPS, LISTED)
    labels = labels.at[:, :, 2].set(jnp.roll(labels[:, :, 2], -1, axis=0)).reshape(-1)

    smem = pl.BlockSpec(memory_space=pltpu.SMEM)
    vmem = pl.BlockSpec(memory_space=pltpu.VMEM)
    partials = pl.pallas_call(
        product_kernel,
        out_shape=jax.ShapeDtypeStruct((parts, PAIRS * slab, BRICK), jnp.bfloat16),
        in_specs=[smem, smem, vmem, vmem, vmem, vmem],
        out_specs=vmem,
        compiler_params=pltpu.CompilerParams(vmem_limit_bytes=32 * 2**20),
        name="products",
    )(left_ids, right_ids, weight.T, own, second, fourth)
    got = exchanged(partials, PLANE)
    sums = pl.pallas_call(
        sum_kernel,
        out_shape=jax.ShapeDtypeStruct((tiles * slab, BRICK), jnp.bfloat16),
        in_specs=[smem, vmem],
        out_specs=vmem,
        scratch_shapes=[pltpu.VMEM((tiles, slab, BRICK), jnp.float32)],
        compiler_params=pltpu.CompilerParams(vmem_limit_bytes=32 * 2**20),
        name="sums",
    )(labels, got)
    sums = exchanged(sums, "mp").reshape(owners, TILES_DEV, slab, BRICK)
    return jnp.sum(sums.astype(jnp.float32), axis=0)


def solution(mesh):
    in_specs = (
        P("tx", ("mp", "rep"), None),
        P(None, "tx", ("mp", "rep")),
        P("tx", ("mp", "rep"), None),
        P("tx", ("mp", "rep"), None),
        P("tx", ("mp", "rep"), None),
    )
    out_specs = P("mp", ("tx", "rep"), None)
    return jax.shard_map(body, mesh=mesh, in_specs=in_specs, out_specs=out_specs, check_vma=False)
```

```python
import functools

import jax
import jax.numpy as jnp
from jax import lax
from jax.experimental import pallas as pl
from jax.experimental.pallas import tpu as pltpu
from jax.sharding import Mesh, PartitionSpec as P

BRICK = 256
STEPS = 4
LISTED = 6
PAIRS = STEPS * LISTED
TILES_DEV = 8
HALVES = 2
GROUP = ("mp_lo", "tx", "rep")
OWNERS = ("mp_hi", "mp_lo")


def exchanged(block, axis):
    return lax.all_to_all(block, axis, split_axis=0, concat_axis=0, tiled=True)


def routes(devices):
    everyone = range(devices)
    swap = [(i ^ 1, i) for i in everyone]
    near = [((i + (1 if i % 2 else 3)) % devices, i) for i in everyone]
    far = [((i + (3 if i % 4 == 1 else -4)) % devices, i) for i in everyone if i % 2]
    return swap, near, far


def product_kernel(chosen, left_ids, right_ids, weight, own, swapped, near, far, out, held, sems):
    copies = [
        pltpu.make_async_copy(block, held.at[i], sems.at[i])
        for i, block in enumerate((own, swapped, near, far))
    ]
    for copy in copies:
        copy.start()
    parts, rows, _ = out.shape
    half = parts // HALVES
    slab = rows // PAIRS
    width = BRICK // HALVES

    def brick(block, index):
        return held[block, :, pl.ds(pl.multiple_of(index * BRICK, BRICK), BRICK)]

    for first in range(0, PAIRS, 2):
        step = first // LISTED
        if first == 0:
            copies[0].wait()
        elif first == LISTED:
            for copy in copies[1:]:
                copy.wait()
        left_block = 0 if step == 0 else chosen[step]
        right_block = 0 if step == 0 else chosen[STEPS + step]
        pair = []
        for entry in (first, first + 1):
            left = brick(left_block, left_ids[entry]).astype(jnp.float32) * weight[:, step : step + 1]
            tile = lax.dot_general(
                left.astype(jnp.bfloat16),
                brick(right_block, right_ids[entry]),
                (((0,), (0,)), ((), ())),
                preferred_element_type=jnp.float32,
            )
            pair.append(tile.reshape(half, slab, BRICK))
        both = jnp.concatenate(pair, axis=1).astype(jnp.bfloat16)
        for side in range(HALVES):
            out[side * half : (side + 1) * half, first * slab : (first + 2) * slab, :] = both[
                :, :, side * width : (side + 1) * width
            ]


def sum_kernel(subsets, labels, got, out, total):
    parts, rows, _ = got.shape
    slab = rows // PAIRS
    plane = parts // HALVES
    total[...] = jnp.zeros_like(total)

    def one_part(part, carry):
        place = part // subsets % 4
        swapped = part + jnp.where(place % 2 == 0, subsets, -subsets)
        earlier = jnp.where(part % plane < 4 * subsets, part + plane - 4 * subsets, part - 4 * subsets)
        listed = (part, part, swapped, jnp.where(place == 3, earlier, part))
        for first in range(0, PAIRS, 2):
            start = listed[first // LISTED] * PAIRS + first
            both = got[part, first * slab : (first + 2) * slab, :].astype(jnp.float32)
            for side in range(2):
                tile = labels[start + side]
                total[tile] += both[side * slab : (side + 1) * slab]
        return carry

    lax.fori_loop(0, parts, one_part, 0)
    out[...] = total[...].reshape(out.shape).astype(out.dtype)


def body(jacobian, coupling, brick_left, brick_right, tile_target):
    own = jacobian[0]
    rows = own.shape[0]
    devices = lax.axis_size("tx")
    swap, near, far = routes(devices)
    place = lax.axis_index("tx") % 4
    parts = devices * lax.axis_size("rep") * HALVES
    owners = lax.axis_size("mp_hi") * lax.axis_size("mp_lo")
    slab = BRICK // (parts // HALVES)
    width = BRICK // HALVES
    tiles = owners * TILES_DEV

    near_block = lax.ppermute(own, "tx", near)
    far_block = lax.ppermute(own, "tx", far)
    swapped_block = lax.ppermute(own, "tx", swap)

    weight = coupling[:, 0]
    ids = jnp.concatenate([brick_left[0, 0], brick_right[0, 0]]).reshape(2, STEPS, LISTED)
    meta = jnp.concatenate([weight[2:], ids[:, 2:].transpose(1, 0, 2).reshape(2, -1).astype(jnp.float32)], axis=1)
    of_swapped = lax.ppermute(meta[0], "tx", swap)
    of_far = jnp.where(place == 3, lax.ppermute(meta[1], "tx", far), meta[1])
    meta = jnp.stack([of_swapped, of_far])
    weight = jnp.concatenate([weight[:2], meta[:, :rows]], axis=0)
    ids = jnp.concatenate(
        [ids[:, :2], meta[:, rows:].astype(jnp.int32).reshape(2, 2, LISTED).transpose(1, 0, 2)], axis=1
    )
    odd = place % 2
    chosen = [0, 0, 1, jnp.where(place == 3, 3, 0)] + [
        0,
        1 + odd,
        2,
        jnp.where(odd == 0, 2, jnp.where(place == 1, 3, 1)),
    ]
    chosen = jnp.stack([jnp.asarray(c, jnp.int32) for c in chosen])

    labels = exchanged(jnp.broadcast_to(tile_target[0], (parts, PAIRS)), GROUP)
    labels = labels.reshape(-1)

    smem = pl.BlockSpec(memory_space=pltpu.SMEM)
    vmem = pl.BlockSpec(memory_space=pltpu.VMEM)
    hbm = pl.BlockSpec(memory_space=pl.ANY)
    partials = pl.pallas_call(
        product_kernel,
        out_shape=jax.ShapeDtypeStruct((parts, PAIRS * slab, width), jnp.bfloat16),
        in_specs=[smem, smem, smem, vmem, hbm, hbm, hbm, hbm],
        out_specs=vmem,
        scratch_shapes=[pltpu.VMEM((4,) + own.shape, own.dtype), pltpu.SemaphoreType.DMA((4,))],
        compiler_params=pltpu.CompilerParams(vmem_limit_bytes=32 * 2**20),
        name="products",
    )(chosen, ids[0].reshape(-1), ids[1].reshape(-1), weight.T, own, swapped_block, near_block, far_block)
    got = exchanged(partials, GROUP)
    sums = pl.pallas_call(
        functools.partial(sum_kernel, lax.axis_size("rep")),
        out_shape=jax.ShapeDtypeStruct((tiles * slab, width), jnp.bfloat16),
        in_specs=[smem, vmem],
        out_specs=vmem,
        scratch_shapes=[pltpu.VMEM((tiles, slab, width), jnp.float32)],
        compiler_params=pltpu.CompilerParams(vmem_limit_bytes=32 * 2**20),
        name="sums",
    )(labels, got)
    sums = exchanged(sums, OWNERS).reshape(owners // HALVES, HALVES, TILES_DEV, slab, width)
    sums = jnp.sum(sums.astype(jnp.float32), axis=0)
    return jnp.concatenate([sums[side] for side in range(HALVES)], axis=-1)


def solution(mesh):
    shape = (mesh.shape["tx"], mesh.shape["mp"] // HALVES, HALVES, mesh.shape["rep"])
    mesh = Mesh(mesh.devices.reshape(shape), ("tx", "mp_hi", "mp_lo", "rep"))
    data = ("mp_hi", "mp_lo", "rep")
    in_specs = (
        P("tx", data, None),
        P(None, "tx", data),
        P("tx", data, None),
        P("tx", data, None),
        P("tx", data, None),
    )
    out_specs = P(OWNERS, ("tx", "rep"), None)
    return jax.shard_map(body, mesh=mesh, in_specs=in_specs, out_specs=out_specs, check_vma=False)
```

```python
import functools

import jax
import jax.numpy as jnp
from jax import lax
from jax.experimental import pallas as pl
from jax.experimental.pallas import tpu as pltpu
from jax.sharding import Mesh, PartitionSpec as P

BRICK = 256
STEPS = 4
LISTED = 6
PAIRS = STEPS * LISTED
TILES_DEV = 8
HALVES = 2
CHAINS = 4
GROUP = ("mp_lo", "tx", "rep")
OWNERS = ("mp_hi", "mp_lo")


def exchanged(block, axis):
    return lax.all_to_all(block, axis, split_axis=0, concat_axis=0, tiled=True)


def routes(devices):
    everyone = range(devices)
    swap = [(i ^ 1, i) for i in everyone]
    near = [((i + (1 if i % 2 else 3)) % devices, i) for i in everyone]
    far = [((i + (3 if i % 4 == 1 else -4)) % devices, i) for i in everyone if i % 2]
    return swap, near, far


def add_tiles(left_ids, right_ids, step, weight, left_block, right_block, out, offset):
    parts = out.shape[0]
    half = parts // HALVES
    slab = BRICK // half
    width = BRICK // HALVES

    def brick(block, index):
        return block[:, pl.ds(pl.multiple_of(index * BRICK, BRICK), BRICK)]

    for first in range(0, LISTED, 2):
        pair = []
        for entry in (first, first + 1):
            left = brick(left_block, left_ids[step * LISTED + entry]).astype(jnp.float32) * weight
            tile = lax.dot_general(
                left.astype(jnp.bfloat16),
                brick(right_block, right_ids[step * LISTED + entry]),
                (((0,), (0,)), ((), ())),
                preferred_element_type=jnp.float32,
            )
            pair.append(tile.reshape(half, slab, BRICK))
        both = jnp.concatenate(pair, axis=1).astype(jnp.bfloat16)
        rows = slice(offset + first * slab, offset + (first + 2) * slab)
        for side in range(HALVES):
            out[side * half : (side + 1) * half, rows, :] = both[:, :, side * width : (side + 1) * width]


def own_kernel(left_ids, right_ids, weight, own, out):
    add_tiles(left_ids, right_ids, 0, weight[...], own, own, out, 0)


def pair_kernel(place, left_ids, right_ids, weight, own, near, far, swapped, out, stage, sems):
    rows = out.shape[1] // (STEPS - 1)
    spot = place[0]
    even = spot % 2 == 0
    cases = (
        ((even, own, swapped), (jnp.logical_not(even), own, near)),
        ((None, swapped, near),),
        ((even, own, near), (spot == 1, own, far), (spot == 3, far, swapped)),
    )
    copies = []
    for step in range(1, STEPS):
        offset = (step - 1) * rows
        for when, left_block, right_block in cases[step - 1]:
            run = functools.partial(
                add_tiles, left_ids, right_ids, step, weight[:, step : step + 1], left_block, right_block, stage, offset
            )
            if when is None:
                run()
            else:
                pl.when(when)(run)
        done = pl.ds(offset, rows)
        copy = pltpu.make_async_copy(stage.at[:, done, :], out.at[:, done, :], sems.at[step - 1])
        copy.start()
        copies.append(copy)
    for copy in copies:
        copy.wait()


def sum_kernel(subsets, first_step, last_step, labels, got, *refs):
    before, out, totals = refs[:-CHAINS - 1], refs[-CHAINS - 1], refs[-CHAINS:]
    parts = got.shape[0]
    plane = parts // HALVES
    slab = totals[0].shape[1]
    for total in totals:
        total[...] = jnp.zeros_like(total)

    def one_part(part, carry):
        place = part // subsets % 4
        swapped = part + jnp.where(place % 2 == 0, subsets, -subsets)
        earlier = jnp.where(part % plane < 4 * subsets, part + plane - 4 * subsets, part - 4 * subsets)
        listed = (part, part, swapped, jnp.where(place == 3, earlier, part))
        for first in range(first_step * LISTED, last_step * LISTED, 2):
            start = listed[first // LISTED] * PAIRS + first
            row = (first - first_step * LISTED) * slab
            both = got[part, row : row + 2 * slab, :].astype(jnp.float32)
            for side in range(2):
                total = totals[(first + side) % CHAINS]
                total[labels[start + side]] += both[side * slab : (side + 1) * slab]
        return carry

    lax.fori_loop(0, parts, one_part, 0)
    whole = functools.reduce(lambda a, b: a + b, [total[...] for total in totals])
    if before:
        whole += before[0][...]
    out[...] = whole.reshape(out.shape).astype(out.dtype)


def body(jacobian, coupling, brick_left, brick_right, tile_target):
    own = jacobian[0]
    rows = own.shape[0]
    devices = lax.axis_size("tx")
    subsets = lax.axis_size("rep")
    swap, near, far = routes(devices)
    place = lax.axis_index("tx") % 4
    parts = devices * subsets * HALVES
    owners = lax.axis_size("mp_hi") * lax.axis_size("mp_lo")
    slab = BRICK // (parts // HALVES)
    width = BRICK // HALVES
    tiles = owners * TILES_DEV
    smem = pl.BlockSpec(memory_space=pltpu.SMEM)
    vmem = pl.BlockSpec(memory_space=pltpu.VMEM)
    params = pltpu.CompilerParams(vmem_limit_bytes=32 * 2**20)

    near_block = lax.ppermute(own, "tx", near)
    far_block = lax.ppermute(own, "tx", far)
    swapped_block = lax.ppermute(own, "tx", swap)
    weight = coupling[:, 0]
    left_ids, right_ids = brick_left[0, 0], brick_right[0, 0]
    cut = 2 * LISTED
    ids = [x[cut:].reshape(2, LISTED) for x in (left_ids, right_ids)]
    meta = jnp.concatenate([weight[2:]] + [x.astype(jnp.float32) for x in ids], axis=1)
    of_swapped = lax.ppermute(meta[0], "tx", swap)
    of_far = jnp.where(place == 3, lax.ppermute(meta[1], "tx", far), meta[1])

    early = pl.pallas_call(
        own_kernel,
        out_shape=jax.ShapeDtypeStruct((parts, LISTED * slab, width), jnp.bfloat16),
        in_specs=[smem, smem, vmem, vmem],
        out_specs=vmem,
        compiler_params=params,
        name="own_products",
    )(left_ids, right_ids, weight[0][:, None], own)
    listed = jnp.pad(tile_target[0].astype(jnp.bfloat16), ((0, slab - 1), (0, width - PAIRS)))
    early = jnp.concatenate([early, jnp.broadcast_to(listed, (parts, slab, width))], axis=1)
    early = exchanged(early, GROUP)
    labels = early[:, LISTED * slab, :PAIRS].astype(jnp.int32).reshape(-1)

    meta = jnp.stack([of_swapped, of_far])
    weight = jnp.concatenate([weight[:2], meta[:, :rows]], axis=0)
    ids = meta[:, rows:].astype(jnp.int32).reshape(2, 2, LISTED)
    left_ids = jnp.concatenate([left_ids[:cut], ids[:, 0].reshape(-1)])
    right_ids = jnp.concatenate([right_ids[:cut], ids[:, 1].reshape(-1)])
    late_shape = (parts, (STEPS - 1) * LISTED * slab, width)
    late = pl.pallas_call(
        pair_kernel,
        out_shape=jax.ShapeDtypeStruct(late_shape, jnp.bfloat16),
        in_specs=[smem, smem, smem, vmem, vmem, vmem, vmem, vmem],
        out_specs=pl.BlockSpec(memory_space=pltpu.HBM),
        scratch_shapes=[pltpu.VMEM(late_shape, jnp.bfloat16), pltpu.SemaphoreType.DMA((STEPS - 1,))],
        compiler_params=params,
        name="pair_products",
    )(place.reshape(1), left_ids, right_ids, weight.T, own, near_block, far_block, swapped_block)
    late = exchanged(late, GROUP)

    chains = [pltpu.VMEM((tiles, slab, width), jnp.float32) for _ in range(CHAINS)]
    first_sums = pl.pallas_call(
        functools.partial(sum_kernel, subsets, 0, 1),
        out_shape=jax.ShapeDtypeStruct((tiles, slab, width), jnp.float32),
        in_specs=[smem, vmem],
        out_specs=vmem,
        scratch_shapes=chains,
        compiler_params=params,
        name="own_sums",
    )(labels, early)
    sums = pl.pallas_call(
        functools.partial(sum_kernel, subsets, 1, STEPS),
        out_shape=jax.ShapeDtypeStruct((tiles * slab, width), jnp.bfloat16),
        in_specs=[smem, vmem, vmem],
        out_specs=vmem,
        scratch_shapes=chains,
        compiler_params=params,
        name="pair_sums",
    )(labels, late, first_sums)
    sums = exchanged(sums, OWNERS).reshape(owners // HALVES, HALVES, TILES_DEV, slab, width)
    sums = jnp.sum(sums.astype(jnp.float32), axis=0)
    return jnp.concatenate([sums[side] for side in range(HALVES)], axis=-1)


def solution(mesh):
    shape = (mesh.shape["tx"], mesh.shape["mp"] // HALVES, HALVES, mesh.shape["rep"])
    mesh = Mesh(mesh.devices.reshape(shape), ("tx", "mp_hi", "mp_lo", "rep"))
    data = ("mp_hi", "mp_lo", "rep")
    in_specs = (
        P("tx", data, None),
        P(None, "tx", data),
        P("tx", data, None),
        P("tx", data, None),
        P("tx", data, None),
    )
    out_specs = P(OWNERS, ("tx", "rep"), None)
    return jax.shard_map(body, mesh=mesh, in_specs=in_specs, out_specs=out_specs, check_vma=False)
```

```python
import functools

import jax
import jax.numpy as jnp
from jax import lax
from jax.experimental import pallas as pl
from jax.experimental.pallas import tpu as pltpu
from jax.sharding import Mesh, PartitionSpec as P

BRICK = 256
STEPS = 4
LISTED = 6
PAIRS = STEPS * LISTED
TILES_DEV = 8
HALVES = 2
CHAINS = 4
GROUP = ("mp_lo", "tx", "rep")
OWNERS = ("mp_hi", "mp_lo")


def exchanged(block, axis):
    return lax.all_to_all(block, axis, split_axis=0, concat_axis=0, tiled=True)


def routes(devices):
    everyone = range(devices)
    swap = [(i ^ 1, i) for i in everyone]
    near = [((i + (1 if i % 2 else 3)) % devices, i) for i in everyone]
    far = [((i + (3 if i % 4 == 1 else -4)) % devices, i) for i in everyone if i % 2]
    return swap, near, far


def add_tiles(left_ids, right_ids, step, weight, left_block, right_block, out, offset):
    parts = out.shape[0]
    half = parts // HALVES
    slab = BRICK // half
    width = BRICK // HALVES

    def brick(block, index):
        return block[:, pl.ds(pl.multiple_of(index * BRICK, BRICK), BRICK)]

    for first in range(0, LISTED, 2):
        pair = []
        for entry in (first, first + 1):
            left = brick(left_block, left_ids[step * LISTED + entry]).astype(jnp.float32) * weight
            tile = lax.dot_general(
                left.astype(jnp.bfloat16),
                brick(right_block, right_ids[step * LISTED + entry]),
                (((0,), (0,)), ((), ())),
                preferred_element_type=jnp.float32,
            )
            pair.append(tile.reshape(half, slab, BRICK))
        both = jnp.concatenate(pair, axis=1).astype(jnp.bfloat16)
        rows = slice(offset + first * slab, offset + (first + 2) * slab)
        for side in range(HALVES):
            out[side * half : (side + 1) * half, rows, :] = both[:, :, side * width : (side + 1) * width]


def own_kernel(left_ids, right_ids, weight, own, out):
    add_tiles(left_ids, right_ids, 0, weight[...], own, own, out, 0)


def pair_kernel(place, left_ids, right_ids, weight, own, near, far, swapped, out, stage, sems):
    rows = out.shape[1] // (STEPS - 1)
    spot = place[0]
    even = spot % 2 == 0
    cases = (
        ((even, own, swapped), (jnp.logical_not(even), own, near)),
        ((None, swapped, near),),
        ((even, own, near), (spot == 1, own, far), (spot == 3, far, swapped)),
    )
    copies = []
    for step in range(1, STEPS):
        offset = (step - 1) * rows
        for when, left_block, right_block in cases[step - 1]:
            run = functools.partial(
                add_tiles, left_ids, right_ids, step, weight[:, step : step + 1], left_block, right_block, stage, offset
            )
            if when is None:
                run()
            else:
                pl.when(when)(run)
        done = pl.ds(offset, rows)
        copy = pltpu.make_async_copy(stage.at[:, done, :], out.at[:, done, :], sems.at[step - 1])
        copy.start()
        copies.append(copy)
    for copy in copies:
        copy.wait()


def sum_kernel(subsets, first_step, last_step, labels, got, *refs):
    before, out, totals = refs[:-CHAINS - 1], refs[-CHAINS - 1], refs[-CHAINS:]
    parts = got.shape[0]
    plane = parts // HALVES
    slab = totals[0].shape[1]
    for total in totals:
        total[...] = jnp.zeros_like(total)

    def one_part(part, carry):
        place = part // subsets % 4
        swapped = part + jnp.where(place % 2 == 0, subsets, -subsets)
        earlier = jnp.where(part % plane < 4 * subsets, part + plane - 4 * subsets, part - 4 * subsets)
        listed = (part, part, swapped, jnp.where(place == 3, earlier, part))
        for first in range(first_step * LISTED, last_step * LISTED, 2):
            start = listed[first // LISTED] * PAIRS + first
            row = (first - first_step * LISTED) * slab
            both = got[part, row : row + 2 * slab, :].astype(jnp.float32)
            for side in range(2):
                total = totals[(first + side) % CHAINS]
                total[labels[start + side]] += both[side * slab : (side + 1) * slab]
        return carry

    lax.fori_loop(0, parts, one_part, 0)
    whole = functools.reduce(lambda a, b: a + b, [total[...] for total in totals])
    if before:
        whole += before[0][...]
    out[...] = whole.reshape(out.shape).astype(out.dtype)


def body(jacobian, coupling, brick_left, brick_right, tile_target):
    own = jacobian[0]
    rows = own.shape[0]
    devices = lax.axis_size("tx")
    subsets = lax.axis_size("rep")
    swap, near, far = routes(devices)
    place = lax.axis_index("tx") % 4
    parts = devices * subsets * HALVES
    owners = lax.axis_size("mp_hi") * lax.axis_size("mp_lo")
    slab = BRICK // (parts // HALVES)
    width = BRICK // HALVES
    tiles = owners * TILES_DEV
    smem = pl.BlockSpec(memory_space=pltpu.SMEM)
    vmem = pl.BlockSpec(memory_space=pltpu.VMEM)
    params = pltpu.CompilerParams(vmem_limit_bytes=32 * 2**20)

    near_block = lax.ppermute(own, "tx", near)
    far_block = lax.ppermute(own, "tx", far)
    swapped_block = lax.ppermute(own, "tx", swap)
    weight = coupling[:, 0]
    left_ids, right_ids = brick_left[0, 0], brick_right[0, 0]
    cut = 2 * LISTED
    ids = [x[cut:].reshape(2, LISTED) for x in (left_ids, right_ids)]
    meta = jnp.concatenate([weight[2:]] + [x.astype(jnp.float32) for x in ids], axis=1)
    of_swapped = lax.ppermute(meta[0], "tx", swap)
    of_far = jnp.where(place == 3, lax.ppermute(meta[1], "tx", far), meta[1])

    early = pl.pallas_call(
        own_kernel,
        out_shape=jax.ShapeDtypeStruct((parts, LISTED * slab, width), jnp.bfloat16),
        in_specs=[smem, smem, vmem, vmem],
        out_specs=vmem,
        compiler_params=params,
        name="own_products",
    )(left_ids, right_ids, weight[0][:, None], own)
    listed = jnp.pad(tile_target[0].astype(jnp.bfloat16), ((0, slab - 1), (0, width - PAIRS)))
    early = jnp.concatenate([early, jnp.broadcast_to(listed, (parts, slab, width))], axis=1)
    early = exchanged(early, GROUP)
    labels = early[:, LISTED * slab, :PAIRS].astype(jnp.int32).reshape(-1)

    meta = jnp.stack([of_swapped, of_far])
    weight = jnp.concatenate([weight[:2], meta[:, :rows]], axis=0)
    ids = meta[:, rows:].astype(jnp.int32).reshape(2, 2, LISTED)
    left_ids = jnp.concatenate([left_ids[:cut], ids[:, 0].reshape(-1)])
    right_ids = jnp.concatenate([right_ids[:cut], ids[:, 1].reshape(-1)])
    late_shape = (parts, (STEPS - 1) * LISTED * slab, width)
    late = pl.pallas_call(
        pair_kernel,
        out_shape=jax.ShapeDtypeStruct(late_shape, jnp.bfloat16),
        in_specs=[smem, smem, smem, vmem, vmem, vmem, vmem, vmem],
        out_specs=pl.BlockSpec(memory_space=pltpu.HBM),
        scratch_shapes=[pltpu.VMEM(late_shape, jnp.bfloat16), pltpu.SemaphoreType.DMA((STEPS - 1,))],
        compiler_params=params,
        cost_estimate=pl.CostEstimate(flops=10**11, bytes_accessed=2**23, transcendentals=0),
        name="pair_products",
    )(place.reshape(1), left_ids, right_ids, weight.T, own, near_block, far_block, swapped_block)
    late = exchanged(late, GROUP)

    chains = [pltpu.VMEM((tiles, slab, width), jnp.float32) for _ in range(CHAINS)]
    first_sums = pl.pallas_call(
        functools.partial(sum_kernel, subsets, 0, 1),
        out_shape=jax.ShapeDtypeStruct((tiles, slab, width), jnp.float32),
        in_specs=[smem, vmem],
        out_specs=vmem,
        scratch_shapes=chains,
        compiler_params=params,
        name="own_sums",
    )(labels, early)
    sums = pl.pallas_call(
        functools.partial(sum_kernel, subsets, 1, STEPS),
        out_shape=jax.ShapeDtypeStruct((tiles * slab, width), jnp.bfloat16),
        in_specs=[smem, vmem, vmem],
        out_specs=vmem,
        scratch_shapes=chains,
        compiler_params=params,
        name="pair_sums",
    )(labels, late, first_sums)
    sums = exchanged(sums, OWNERS).reshape(owners // HALVES, HALVES, TILES_DEV, slab, width)
    sums = jnp.sum(sums.astype(jnp.float32), axis=0)
    return jnp.concatenate([sums[side] for side in range(HALVES)], axis=-1)


def solution(mesh):
    shape = (mesh.shape["tx"], mesh.shape["mp"] // HALVES, HALVES, mesh.shape["rep"])
    mesh = Mesh(mesh.devices.reshape(shape), ("tx", "mp_hi", "mp_lo", "rep"))
    data = ("mp_hi", "mp_lo", "rep")
    in_specs = (
        P("tx", data, None),
        P(None, "tx", data),
        P("tx", data, None),
        P("tx", data, None),
        P("tx", data, None),
    )
    out_specs = P(OWNERS, ("tx", "rep"), None)
    return jax.shard_map(body, mesh=mesh, in_specs=in_specs, out_specs=out_specs, check_vma=False)
```

```python
import functools

import jax
import jax.numpy as jnp
from jax import lax
from jax.experimental import pallas as pl
from jax.experimental.pallas import tpu as pltpu
from jax.sharding import Mesh, PartitionSpec as P

BRICK = 256
STEPS = 4
LISTED = 6
PAIRS = STEPS * LISTED
TILES_DEV = 8
HALVES = 2
COST = 10**11
GROUP = ("mp_lo", "tx", "rep")
OWNERS = ("mp_hi", "mp_lo")


def exchanged(block, axis):
    return lax.all_to_all(block, axis, split_axis=0, concat_axis=0, tiled=True)


def routes(devices):
    everyone = range(devices)
    swap = [(i ^ 1, i) for i in everyone]
    near = [((i + (1 if i % 2 else 3)) % devices, i) for i in everyone]
    far = [((i + (3 if i % 4 == 1 else -4)) % devices, i) for i in everyone if i % 2]
    return swap, near, far


def column(row):
    return jnp.broadcast_to(row, (BRICK, row.shape[1])).T


def column(row):
    return jnp.broadcast_to(row, (BRICK, row.shape[1])).T


def add_tiles(left_ids, right_ids, weight, left_block, right_block, out, slot, then=None):
    parts = out.shape[0]
    half = parts // HALVES
    slab = BRICK // half
    width = BRICK // HALVES

    def brick(block, index):
        return block[:, pl.ds(pl.multiple_of(index * BRICK, BRICK), BRICK)]

    for first in range(0, LISTED, 2):
        pair = []
        for entry in (first, first + 1):
            left = brick(left_block, left_ids(entry)).astype(jnp.float32) * weight
            tile = lax.dot_general(
                left.astype(jnp.bfloat16),
                brick(right_block, right_ids(entry)),
                (((0,), (0,)), ((), ())),
                preferred_element_type=jnp.float32,
            )
            pair.append(tile.reshape(half, slab, BRICK))
        both = jnp.concatenate(pair, axis=1).astype(jnp.bfloat16)
        row = (slot * LISTED + first) * slab
        for side in range(HALVES):
            out[side * half : (side + 1) * half, row : row + 2 * slab, :] = both[
                :, :, side * width : (side + 1) * width
            ]
        if then is not None:
            then(row, 2 * slab)


def fetched(pairs, sems):
    copies = [pltpu.make_async_copy(src, dst, sems.at[i]) for i, (src, dst) in enumerate(pairs)]
    for copy in copies:
        copy.start()
    return copies


def own_kernel(*refs):
    place, left_hbm, right_hbm, targets_hbm, coupling_hbm, whole, out, own, *metas = refs[:11]
    left_ids, right_ids, lists, targets, coupling, numbers, sems = refs[11:]
    pairs = (
        (left_hbm, left_ids),
        (right_hbm, right_ids),
        (left_hbm, lists.at[0]),
        (right_hbm, lists.at[1]),
        (targets_hbm, targets),
        (coupling_hbm, coupling),
        (whole.at[0], own),
    )
    for copy in fetched(pairs, sems):
        copy.wait()
    rows = own.shape[0]
    for step, meta in enumerate(metas, 1):
        here = slice(step * LISTED, (step + 1) * LISTED)
        meta[...] = jnp.zeros_like(meta)
        meta[0:1, 0:rows] = coupling[step]
        for side in range(2):
            first = rows + side * LISTED
            meta[0:1, first : first + LISTED] = lists[side, 0, :, here].astype(jnp.float32)
    even = place[0] % 2 == 0
    numbers[...] = jnp.zeros_like(numbers)
    for slot, other in enumerate((0, 3, 2, 1)):
        these, those = (targets[0, :, i * LISTED : (i + 1) * LISTED] for i in (slot, other))
        here = slice(slot * LISTED, (slot + 1) * LISTED)
        numbers[0:1, here] = jnp.where(even, those, these).astype(jnp.float32)
    slab = numbers.shape[0]
    below = jnp.broadcast_to(numbers[...].astype(jnp.bfloat16)[None], (out.shape[0],) + numbers.shape)
    out[:, 2 * LISTED * slab :, :] = below
    add_tiles(lambda i: left_ids[0, 0, i], lambda i: right_ids[0, 0, i], column(coupling[0]), own, own, out, 0)


def pair_of(metas, lists, slot, rows, *blocks_and_out):
    first = slot * 2 * LISTED
    weight = column(metas[slot : slot + 1, 0:rows])
    return (lambda i: lists[first + i], lambda i: lists[first + LISTED + i], weight) + blocks_and_out


def last_kernel(lists, metas, own, far, swapped, _, out, stage, sems):
    rows = own.shape[0]
    height = stage.shape[1]
    spot = lists[2 * LISTED]

    def run(left_block, right_block):
        copies = []

        def send(row, size):
            part = stage.at[:, pl.ds(row, size), :]
            copies.append(
                pltpu.make_async_copy(part, out.at[:, pl.ds(height + row, size), :], sems.at[len(copies)])
            )
            copies[-1].start()

        add_tiles(*pair_of(metas, lists, 0, rows, left_block, right_block, stage, 0), send)
        for copy in copies:
            copy.wait()

    pl.when(spot % 2 == 0)(lambda: run(own, swapped))
    pl.when(spot == 1)(lambda: run(own, far))
    pl.when(spot == 3)(lambda: run(far, swapped))


def near_kernel(lists, metas, whole, swapped, near, out, own, sems):
    (load,) = fetched([(whole.at[0], own)], sems)
    rows = own.shape[0]
    add_tiles(*pair_of(metas, lists, 1, rows, swapped, near, out, 1))
    load.wait()
    add_tiles(*pair_of(metas, lists, 0, rows, own, near, out, 0))


def add_up(labels, starts, got, part, totals):
    slab = totals[0].shape[1]
    for slot, start in enumerate(starts):
        for first in range(0, LISTED, 2):
            row = (slot * LISTED + first) * slab
            both = got[part, row : row + 2 * slab, :].astype(jnp.float32)
            for side in range(2):
                total = totals[first + side]
                total[labels[start + first + side]] += both[side * slab : (side + 1) * slab]


def together(totals):
    return functools.reduce(lambda a, b: a + b, [total[...] for total in totals])


def first_sum_kernel(subsets, labels, got, out, *totals):
    parts = got.shape[0]
    plane = parts // HALVES
    for total in totals:
        total[...] = jnp.zeros_like(total)

    def one_part(part, carry):
        earlier = jnp.where(part % plane < 4 * subsets, part + plane - 4 * subsets, part - 4 * subsets)
        lister = jnp.where(part // subsets % 4 == 3, earlier, part)
        add_up(labels, [part * PAIRS, lister * PAIRS + 3 * LISTED], got, part, totals)
        return carry

    lax.fori_loop(0, parts, one_part, 0)
    out[...] = together(totals)


def near_sum_kernel(subsets, labels, got, before, out, held, sems, *totals):
    (load,) = fetched([(before, held)], sems)
    for total in totals:
        total[...] = jnp.zeros_like(total)

    def one_part(part, carry):
        lister = part + jnp.where(part // subsets % 2 == 0, subsets, -subsets)
        add_up(labels, [part * PAIRS + LISTED, lister * PAIRS + 2 * LISTED], got, part, totals)
        return carry

    lax.fori_loop(0, got.shape[0], one_part, 0)
    load.wait()
    out[...] = together((held,) + totals).reshape(out.shape).astype(out.dtype)


def body(jacobian, coupling, brick_left, brick_right, tile_target):
    rows = jacobian.shape[1]
    devices = lax.axis_size("tx")
    subsets = lax.axis_size("rep")
    swap, near, far = routes(devices)
    parts = devices * subsets * HALVES
    owners = lax.axis_size("mp_hi") * lax.axis_size("mp_lo")
    slab = BRICK // (parts // HALVES)
    width = BRICK // HALVES
    tiles = owners * TILES_DEV
    smem = pl.BlockSpec(memory_space=pltpu.SMEM)
    vmem = pl.BlockSpec(memory_space=pltpu.VMEM)
    hbm = pl.BlockSpec(memory_space=pl.ANY)
    params = pltpu.CompilerParams(vmem_limit_bytes=24 * 2**20)
    args = [pltpu.with_memory_space_constraint(x, pltpu.HBM) for x in (brick_left, brick_right, tile_target, coupling)]
    whole = pltpu.with_memory_space_constraint(jacobian, pltpu.HBM)
    held = pltpu.VMEM(jacobian.shape[1:], jacobian.dtype)
    copied = pltpu.SemaphoreType.DMA

    swapped_block = lax.ppermute(jacobian[0], "tx", swap)
    far_block = lax.ppermute(jacobian[0], "tx", far)
    near_block = lax.ppermute(jacobian[0], "tx", near)
    place = lax.axis_index("tx") & 3
    spot = place.reshape(1).astype(jnp.int32)

    first = pltpu.HBM((parts, (2 * LISTED + 1) * slab, width), jnp.bfloat16)
    stage = pltpu.VMEM((parts, LISTED * slab, width), jnp.bfloat16)
    meta = jax.ShapeDtypeStruct((1, rows + width), jnp.float32)
    buffer, own, of_one, of_two, of_three = pl.pallas_call(
        own_kernel,
        out_shape=(first, held, meta, meta, meta),
        in_specs=[smem] + [hbm] * 5,
        out_specs=[vmem] * 5,
        scratch_shapes=[
            pltpu.SMEM(brick_left.shape, jnp.int32),
            pltpu.SMEM(brick_right.shape, jnp.int32),
            pltpu.VMEM((2,) + brick_left.shape, jnp.int32),
            pltpu.VMEM(tile_target.shape, jnp.int32),
            pltpu.VMEM(coupling.shape, coupling.dtype),
            pltpu.VMEM((slab, width), jnp.float32),
            copied((7,)),
        ],
        compiler_params=params,
        name="own_products",
    )(spot, *args, whole)
    of_far = lax.ppermute(of_three, "tx", far)
    of_swapped = lax.ppermute(of_two, "tx", swap)
    even = place % 2 == 0

    def listed(metas):
        return metas[:, rows : rows + 2 * LISTED].astype(jnp.int32).reshape(-1)

    last = jnp.where(even, of_one, jnp.where(place == 1, of_three, of_far))
    buffer = pl.pallas_call(
        last_kernel,
        out_shape=first,
        in_specs=[smem] + [vmem] * 4 + [hbm],
        out_specs=hbm,
        scratch_shapes=[stage, copied((LISTED // 2,))],
        input_output_aliases={5: 0},
        compiler_params=params,
        name="last_products",
    )(jnp.concatenate([listed(last), spot]), last, own, far_block, swapped_block, buffer)
    got = exchanged(buffer, GROUP)
    labels = got[:, 2 * LISTED * slab, :PAIRS].astype(jnp.int32).reshape(-1)

    metas = jnp.concatenate([jnp.where(even, of_three, of_one), of_swapped], axis=0)
    second = pl.pallas_call(
        near_kernel,
        out_shape=jax.ShapeDtypeStruct((parts, 2 * LISTED * slab, width), jnp.bfloat16),
        in_specs=[smem, vmem, hbm, vmem, vmem],
        out_specs=vmem,
        scratch_shapes=[held, copied((1,))],
        compiler_params=params,
        cost_estimate=pl.CostEstimate(flops=COST, bytes_accessed=2**23, transcendentals=0),
        name="near_products",
    )(listed(metas), metas, whole, swapped_block, near_block)
    second = exchanged(second, GROUP)

    chains = [pltpu.VMEM((tiles, slab, width), jnp.float32) for _ in range(LISTED)]
    sums = pl.pallas_call(
        functools.partial(first_sum_kernel, subsets),
        out_shape=jax.ShapeDtypeStruct((tiles, slab, width), jnp.float32),
        in_specs=[smem, vmem],
        out_specs=vmem,
        scratch_shapes=chains,
        compiler_params=params,
        name="first_sums",
    )(labels, got)
    sums = pl.pallas_call(
        functools.partial(near_sum_kernel, subsets),
        out_shape=jax.ShapeDtypeStruct((tiles * slab, width), jnp.bfloat16),
        in_specs=[smem, vmem, hbm],
        out_specs=vmem,
        scratch_shapes=[chains[0], copied((1,))] + chains,
        compiler_params=params,
        name="near_sums",
    )(labels, second, pltpu.with_memory_space_constraint(sums, pltpu.HBM))
    sums = exchanged(sums, OWNERS).reshape(owners // HALVES, HALVES, TILES_DEV, slab, width)
    sums = jnp.sum(sums.astype(jnp.float32), axis=0)
    return jnp.concatenate([sums[side] for side in range(HALVES)], axis=-1)


def solution(mesh):
    shape = (mesh.shape["tx"], mesh.shape["mp"] // HALVES, HALVES, mesh.shape["rep"])
    mesh = Mesh(mesh.devices.reshape(shape), ("tx", "mp_hi", "mp_lo", "rep"))
    data = ("mp_hi", "mp_lo", "rep")
    in_specs = (
        P("tx", data, None),
        P(None, "tx", data),
        P("tx", data, None),
        P("tx", data, None),
        P("tx", data, None),
    )
    out_specs = P(OWNERS, ("tx", "rep"), None)
    return jax.shard_map(body, mesh=mesh, in_specs=in_specs, out_specs=out_specs, check_vma=False)
```

```python
import functools

import jax
import jax.numpy as jnp
from jax import lax
from jax.experimental import pallas as pl
from jax.experimental.pallas import tpu as pltpu
from jax.sharding import Mesh, PartitionSpec as P

BRICK = 256
STEPS = 4
LISTED = 6
PAIRS = STEPS * LISTED
TILES_DEV = 8
HALVES = 2
COST = 10**11
TAIL = 16
GROUP = ("mp_lo", "tx", "rep")
OWNERS = ("mp_hi", "mp_lo")


def exchanged(block, axis):
    return lax.all_to_all(block, axis, split_axis=0, concat_axis=0, tiled=True)


def routes(devices):
    everyone = range(devices)
    swap = [(i ^ 1, i) for i in everyone]
    near = [((i + (1 if i % 2 else 3)) % devices, i) for i in everyone]
    far = [((i + (3 if i % 4 == 1 else -4)) % devices, i) for i in everyone if i % 2]
    return swap, near, far


def column(row):
    return jnp.broadcast_to(row, (BRICK, row.shape[1])).T


def column(row):
    return jnp.broadcast_to(row, (BRICK, row.shape[1])).T


def add_tiles(left_ids, right_ids, weight, left_block, right_block, out, slot, then=None):
    parts = out.shape[0]
    half = parts // HALVES
    slab = BRICK // half
    width = BRICK // HALVES

    def brick(block, index):
        columns = pl.ds(pl.multiple_of(index * BRICK, BRICK), BRICK)
        if not isinstance(block, tuple):
            return block[:, columns]
        top, tail = block
        return jnp.concatenate([top[:, columns], tail[0:TAIL, columns].astype(jnp.bfloat16)], axis=0)

    for first in range(0, LISTED, 2):
        pair = []
        for entry in (first, first + 1):
            left = brick(left_block, left_ids(entry)).astype(jnp.float32) * weight
            tile = lax.dot_general(
                left.astype(jnp.bfloat16),
                brick(right_block, right_ids(entry)),
                (((0,), (0,)), ((), ())),
                preferred_element_type=jnp.float32,
            )
            pair.append(tile.reshape(half, slab, BRICK))
        both = jnp.concatenate(pair, axis=1).astype(jnp.bfloat16)
        row = (slot * LISTED + first) * slab
        for side in range(HALVES):
            out[side * half : (side + 1) * half, row : row + 2 * slab, :] = both[
                :, :, side * width : (side + 1) * width
            ]
        if then is not None:
            then(row, 2 * slab)


def fetched(pairs, sems):
    copies = [pltpu.make_async_copy(src, dst, sems.at[i]) for i, (src, dst) in enumerate(pairs)]
    for copy in copies:
        copy.start()
    return copies


def own_kernel(*refs):
    place, left_hbm, right_hbm, targets_hbm, coupling_hbm, whole, out, own, top, *metas = refs[:12]
    left_ids, right_ids, lists, targets, coupling, numbers, sems = refs[12:]
    pairs = (
        (left_hbm, left_ids),
        (right_hbm, right_ids),
        (left_hbm, lists.at[0]),
        (right_hbm, lists.at[1]),
        (targets_hbm, targets),
        (coupling_hbm, coupling),
        (whole.at[0], own),
    )
    for copy in fetched(pairs, sems):
        copy.wait()
    rows = own.shape[0]
    top[...] = own[: rows - TAIL, :]
    for step, meta in enumerate(metas, 1):
        here = slice(step * LISTED, (step + 1) * LISTED)
        meta[...] = jnp.zeros_like(meta)
        row = meta.shape[0] // (TAIL + 8) * TAIL
        if row > 0:
            meta[0:row, :] = own[rows - row :, :].astype(jnp.float32)
        meta[row : row + 1, 0:rows] = coupling[step]
        for side in range(2):
            first = rows + side * LISTED
            meta[row : row + 1, first : first + LISTED] = lists[side, 0, :, here].astype(jnp.float32)
    even = place[0] % 2 == 0
    numbers[...] = jnp.zeros_like(numbers)
    for slot, other in enumerate((0, 3, 2, 1)):
        these, those = (targets[0, :, i * LISTED : (i + 1) * LISTED] for i in (slot, other))
        here = slice(slot * LISTED, (slot + 1) * LISTED)
        numbers[0:1, here] = jnp.where(even, those, these).astype(jnp.float32)
    slab = numbers.shape[0]
    below = jnp.broadcast_to(numbers[...].astype(jnp.bfloat16)[None], (out.shape[0],) + numbers.shape)
    out[:, 2 * LISTED * slab :, :] = below
    add_tiles(lambda i: left_ids[0, 0, i], lambda i: right_ids[0, 0, i], column(coupling[0]), own, own, out, 0)


def pair_of(metas, lists, slot, rows, *blocks_and_out):
    first = slot * 2 * LISTED
    weight = column(metas[slot : slot + 1, 0:rows])
    return (lambda i: lists[first + i], lambda i: lists[first + LISTED + i], weight) + blocks_and_out


def last_kernel(lists, metas, own, *refs):
    far, swapped, (_, out, stage, sems) = refs[0], refs[1:3], refs[3:]
    rows = own.shape[0]
    height = stage.shape[1]
    spot = lists[2 * LISTED]

    def run(left_block, right_block):
        copies = []

        def send(row, size):
            part = stage.at[:, pl.ds(row, size), :]
            copies.append(
                pltpu.make_async_copy(part, out.at[:, pl.ds(height + row, size), :], sems.at[len(copies)])
            )
            copies[-1].start()

        add_tiles(*pair_of(metas, lists, 0, rows, left_block, right_block, stage, 0), send)
        for copy in copies:
            copy.wait()

    pl.when(spot % 2 == 0)(lambda: run(own, swapped))
    pl.when(spot == 1)(lambda: run(own, far))
    pl.when(spot == 3)(lambda: run(far, swapped))


def near_kernel(lists, metas, whole, top, tail, near, out, own, sems):
    swapped = (top, tail)
    (load,) = fetched([(whole.at[0], own)], sems)
    rows = own.shape[0]
    add_tiles(*pair_of(metas, lists, 1, rows, swapped, near, out, 1))
    load.wait()
    add_tiles(*pair_of(metas, lists, 0, rows, own, near, out, 0))


def add_up(labels, starts, got, part, totals):
    slab = totals[0].shape[1]
    for slot, start in enumerate(starts):
        for first in range(0, LISTED, 2):
            row = (slot * LISTED + first) * slab
            both = got[part, row : row + 2 * slab, :].astype(jnp.float32)
            for side in range(2):
                total = totals[first + side]
                total[labels[start + first + side]] += both[side * slab : (side + 1) * slab]


def together(totals):
    return functools.reduce(lambda a, b: a + b, [total[...] for total in totals])


def first_sum_kernel(subsets, labels, got, out, *totals):
    parts = got.shape[0]
    plane = parts // HALVES
    for total in totals:
        total[...] = jnp.zeros_like(total)

    def one_part(part, carry):
        earlier = jnp.where(part % plane < 4 * subsets, part + plane - 4 * subsets, part - 4 * subsets)
        lister = jnp.where(part // subsets % 4 == 3, earlier, part)
        add_up(labels, [part * PAIRS, lister * PAIRS + 3 * LISTED], got, part, totals)
        return carry

    lax.fori_loop(0, parts, one_part, 0)
    out[...] = together(totals)


def near_sum_kernel(subsets, labels, got, before, out, held, sems, *totals):
    (load,) = fetched([(before, held)], sems)
    for total in totals:
        total[...] = jnp.zeros_like(total)

    def one_part(part, carry):
        lister = part + jnp.where(part // subsets % 2 == 0, subsets, -subsets)
        add_up(labels, [part * PAIRS + LISTED, lister * PAIRS + 2 * LISTED], got, part, totals)
        return carry

    lax.fori_loop(0, got.shape[0], one_part, 0)
    load.wait()
    out[...] = together((held,) + totals).reshape(out.shape).astype(out.dtype)


def body(jacobian, coupling, brick_left, brick_right, tile_target):
    rows = jacobian.shape[1]
    devices = lax.axis_size("tx")
    subsets = lax.axis_size("rep")
    swap, near, far = routes(devices)
    parts = devices * subsets * HALVES
    owners = lax.axis_size("mp_hi") * lax.axis_size("mp_lo")
    slab = BRICK // (parts // HALVES)
    width = BRICK // HALVES
    tiles = owners * TILES_DEV
    smem = pl.BlockSpec(memory_space=pltpu.SMEM)
    vmem = pl.BlockSpec(memory_space=pltpu.VMEM)
    hbm = pl.BlockSpec(memory_space=pl.ANY)
    params = pltpu.CompilerParams(vmem_limit_bytes=24 * 2**20)
    args = [pltpu.with_memory_space_constraint(x, pltpu.HBM) for x in (brick_left, brick_right, tile_target, coupling)]
    whole = pltpu.with_memory_space_constraint(jacobian, pltpu.HBM)
    held = pltpu.VMEM(jacobian.shape[1:], jacobian.dtype)
    copied = pltpu.SemaphoreType.DMA

    near_block = lax.ppermute(jacobian[0], "tx", near)
    far_block = lax.ppermute(jacobian[0], "tx", far)
    place = lax.axis_index("tx") & 3
    spot = place.reshape(1).astype(jnp.int32)

    first = pltpu.HBM((parts, (2 * LISTED + 1) * slab, width), jnp.bfloat16)
    stage = pltpu.VMEM((parts, LISTED * slab, width), jnp.bfloat16)
    meta = jax.ShapeDtypeStruct((1, rows + width), jnp.float32)
    tall = jax.ShapeDtypeStruct((TAIL + 8, jacobian.shape[2]), jnp.float32)
    buffer, own, top, of_one, of_two, of_three = pl.pallas_call(
        own_kernel,
        out_shape=(
            first,
            held,
            jax.ShapeDtypeStruct((rows - TAIL, jacobian.shape[2]), jacobian.dtype),
            meta,
            tall,
            meta,
        ),
        in_specs=[smem] + [hbm] * 5,
        out_specs=[vmem] * 6,
        scratch_shapes=[
            pltpu.SMEM(brick_left.shape, jnp.int32),
            pltpu.SMEM(brick_right.shape, jnp.int32),
            pltpu.VMEM((2,) + brick_left.shape, jnp.int32),
            pltpu.VMEM(tile_target.shape, jnp.int32),
            pltpu.VMEM(coupling.shape, coupling.dtype),
            pltpu.VMEM((slab, width), jnp.float32),
            copied((7,)),
        ],
        compiler_params=params,
        name="own_products",
    )(spot, *args, whole)
    swapped_top = lax.ppermute(top, "tx", swap)
    of_far = lax.ppermute(of_three, "tx", far)
    of_swapped = lax.ppermute(of_two, "tx", swap)
    even = place % 2 == 0

    def meta_row(tail):
        return tail[TAIL : TAIL + 1, : rows + width]

    def listed(metas):
        return metas[:, rows : rows + 2 * LISTED].astype(jnp.int32).reshape(-1)

    last = jnp.where(even, of_one, jnp.where(place == 1, of_three, of_far))
    buffer = pl.pallas_call(
        last_kernel,
        out_shape=first,
        in_specs=[smem] + [vmem] * 5 + [hbm],
        out_specs=hbm,
        scratch_shapes=[stage, copied((LISTED // 2,))],
        input_output_aliases={6: 0},
        compiler_params=params,
        name="last_products",
    )(jnp.concatenate([listed(last), spot]), last, own, far_block, swapped_top, of_swapped, buffer)
    got = exchanged(buffer, GROUP)
    labels = got[:, 2 * LISTED * slab, :PAIRS].astype(jnp.int32).reshape(-1)

    metas = jnp.concatenate([jnp.where(even, of_three, of_one), meta_row(of_swapped)], axis=0)
    second = pl.pallas_call(
        near_kernel,
        out_shape=jax.ShapeDtypeStruct((parts, 2 * LISTED * slab, width), jnp.bfloat16),
        in_specs=[smem, vmem, hbm, vmem, vmem, vmem],
        out_specs=vmem,
        scratch_shapes=[held, copied((1,))],
        compiler_params=params,
        cost_estimate=pl.CostEstimate(flops=COST, bytes_accessed=2**23, transcendentals=0),
        name="near_products",
    )(listed(metas), metas, whole, swapped_top, of_swapped, near_block)
    second = exchanged(second, GROUP)

    chains = [pltpu.VMEM((tiles, slab, width), jnp.float32) for _ in range(LISTED)]
    sums = pl.pallas_call(
        functools.partial(first_sum_kernel, subsets),
        out_shape=jax.ShapeDtypeStruct((tiles, slab, width), jnp.float32),
        in_specs=[smem, vmem],
        out_specs=vmem,
        scratch_shapes=chains,
        compiler_params=params,
        name="first_sums",
    )(labels, got)
    sums = pl.pallas_call(
        functools.partial(near_sum_kernel, subsets),
        out_shape=jax.ShapeDtypeStruct((tiles * slab, width), jnp.bfloat16),
        in_specs=[smem, vmem, hbm],
        out_specs=vmem,
        scratch_shapes=[chains[0], copied((1,))] + chains,
        compiler_params=params,
        name="near_sums",
    )(labels, second, pltpu.with_memory_space_constraint(sums, pltpu.HBM))
    sums = exchanged(sums, OWNERS).reshape(owners // HALVES, HALVES, TILES_DEV, slab, width)
    sums = jnp.sum(sums.astype(jnp.float32), axis=0)
    return jnp.concatenate([sums[side] for side in range(HALVES)], axis=-1)


def solution(mesh):
    shape = (mesh.shape["tx"], mesh.shape["mp"] // HALVES, HALVES, mesh.shape["rep"])
    mesh = Mesh(mesh.devices.reshape(shape), ("tx", "mp_hi", "mp_lo", "rep"))
    data = ("mp_hi", "mp_lo", "rep")
    in_specs = (
        P("tx", data, None),
        P(None, "tx", data),
        P("tx", data, None),
        P("tx", data, None),
        P("tx", data, None),
    )
    out_specs = P(OWNERS, ("tx", "rep"), None)
    return jax.shard_map(body, mesh=mesh, in_specs=in_specs, out_specs=out_specs, check_vma=False)
```

```python
import functools

import jax
import jax.numpy as jnp
from jax import lax
from jax.experimental import pallas as pl
from jax.experimental.pallas import tpu as pltpu
from jax.sharding import Mesh, PartitionSpec as P

BRICK = 256
STEPS = 4
LISTED = 6
PAIRS = STEPS * LISTED
TILES_DEV = 8
HALVES = 2
COST = 10**11
TAIL = 16
GROUP = ("mp_lo", "tx", "rep")
OWNERS = ("mp_hi", "mp_lo")


def exchanged(block, axis):
    return lax.all_to_all(block, axis, split_axis=0, concat_axis=0, tiled=True)


def routes(devices):
    everyone = range(devices)
    swap = [(i ^ 1, i) for i in everyone]
    near = [((i + (1 if i % 2 else 3)) % devices, i) for i in everyone]
    far = [((i + (3 if i % 4 == 1 else -4)) % devices, i) for i in everyone if i % 2]
    return swap, near, far, [(source, to) for source, to in far if to % 4 == 3]


def column(row):
    return jnp.broadcast_to(row, (BRICK, row.shape[1])).T


def column(row):
    return jnp.broadcast_to(row, (BRICK, row.shape[1])).T


def add_tiles(left_ids, right_ids, weight, left_block, right_block, out, slot, then=None):
    parts = out.shape[0]
    half = parts // HALVES
    slab = BRICK // half
    width = BRICK // HALVES

    def brick(block, index):
        columns = pl.ds(pl.multiple_of(index * BRICK, BRICK), BRICK)
        if not isinstance(block, tuple):
            return block[:, columns]
        top, tail = block
        return jnp.concatenate([top[:, columns], tail[0:TAIL, columns].astype(jnp.bfloat16)], axis=0)

    for first in range(0, LISTED, 2):
        pair = []
        for entry in (first, first + 1):
            left = brick(left_block, left_ids(entry)).astype(jnp.float32) * weight
            tile = lax.dot_general(
                left.astype(jnp.bfloat16),
                brick(right_block, right_ids(entry)),
                (((0,), (0,)), ((), ())),
                preferred_element_type=jnp.float32,
            )
            pair.append(tile.reshape(half, slab, BRICK))
        both = jnp.concatenate(pair, axis=1).astype(jnp.bfloat16)
        row = (slot * LISTED + first) * slab
        for side in range(HALVES):
            out[side * half : (side + 1) * half, row : row + 2 * slab, :] = both[
                :, :, side * width : (side + 1) * width
            ]
        if then is not None:
            then(row, 2 * slab)


def quarters(whole, held):
    rows = held.shape[0] // 4
    return [(whole.at[0, pl.ds(i * rows, rows), :], held.at[pl.ds(i * rows, rows), :]) for i in range(4)]


def fetched(pairs, sems):
    copies = [pltpu.make_async_copy(src, dst, sems.at[i]) for i, (src, dst) in enumerate(pairs)]
    for copy in copies:
        copy.start()
    return copies


def own_kernel(*refs):
    place, left_hbm, right_hbm, targets_hbm, coupling_hbm, whole, out, own, top, *metas = refs[:12]
    left_ids, right_ids, lists, targets, coupling, numbers, sems = refs[12:]
    pairs = (
        (left_hbm, left_ids),
        (right_hbm, right_ids),
        (left_hbm, lists.at[0]),
        (right_hbm, lists.at[1]),
        (targets_hbm, targets),
        (coupling_hbm, coupling),
    ) + tuple(quarters(whole, own))
    copies = fetched(pairs, sems)
    for meta in metas:
        meta[...] = jnp.zeros_like(meta)
    numbers[...] = jnp.zeros_like(numbers)
    for copy in copies[:6]:
        copy.wait()
    even = place[0] % 2 == 0
    for slot, other in enumerate((0, 3, 2, 1)):
        these, those = (targets[0, :, i * LISTED : (i + 1) * LISTED] for i in (slot, other))
        here = slice(slot * LISTED, (slot + 1) * LISTED)
        numbers[0:1, here] = jnp.where(even, those, these).astype(jnp.float32)
    slab = numbers.shape[0]
    below = jnp.broadcast_to(numbers[...].astype(jnp.bfloat16)[None], (out.shape[0],) + numbers.shape)
    out[:, 2 * LISTED * slab :, :] = below
    rows = own.shape[0]
    for step, meta in enumerate(metas, 1):
        here = slice(step * LISTED, (step + 1) * LISTED)
        row = meta.shape[0] // (TAIL + 8) * TAIL
        meta[row : row + 1, 0:rows] = coupling[step]
        for side in range(2):
            first = rows + side * LISTED
            meta[row : row + 1, first : first + LISTED] = lists[side, 0, :, here].astype(jnp.float32)
    for copy in copies[6:]:
        copy.wait()
    top[...] = own[: rows - TAIL, :]
    metas[1][0:TAIL, :] = own[rows - TAIL :, :].astype(jnp.float32)
    add_tiles(lambda i: left_ids[0, 0, i], lambda i: right_ids[0, 0, i], column(coupling[0]), own, own, out, 0)


def pair_of(metas, lists, slot, rows, *blocks_and_out):
    first = slot * 2 * LISTED
    weight = column(metas[slot : slot + 1, 0:rows])
    return (lambda i: lists[first + i], lambda i: lists[first + LISTED + i], weight) + blocks_and_out


def last_kernel(lists, metas, own, *refs):
    far, swapped, (_, out, stage, sems) = refs[0], refs[1:3], refs[3:]
    rows = own.shape[0]
    height = stage.shape[1]
    spot = lists[2 * LISTED]

    def run(left_block, right_block):
        copies = []

        def send(row, size):
            part = stage.at[:, pl.ds(row, size), :]
            copies.append(
                pltpu.make_async_copy(part, out.at[:, pl.ds(height + row, size), :], sems.at[len(copies)])
            )
            copies[-1].start()

        add_tiles(*pair_of(metas, lists, 0, rows, left_block, right_block, stage, 0), send)
        for copy in copies:
            copy.wait()

    pl.when(spot % 2 == 0)(lambda: run(own, swapped))
    pl.when(spot == 1)(lambda: run(own, far))
    pl.when(spot == 3)(lambda: run(far, swapped))


def near_kernel(lists, metas, whole, top, tail, near, out, own, sems):
    swapped = (top, tail)
    loads = fetched(quarters(whole, own), sems)
    rows = own.shape[0]
    add_tiles(*pair_of(metas, lists, 1, rows, swapped, near, out, 1))
    for load in loads:
        load.wait()
    add_tiles(*pair_of(metas, lists, 0, rows, own, near, out, 0))


def add_up(labels, starts, got, part, totals):
    slab = totals[0].shape[1]
    for slot, start in enumerate(starts):
        for first in range(0, LISTED, 2):
            row = (slot * LISTED + first) * slab
            both = got[part, row : row + 2 * slab, :].astype(jnp.float32)
            for side in range(2):
                total = totals[first + side]
                total[labels[start + first + side]] += both[side * slab : (side + 1) * slab]


def together(totals):
    return functools.reduce(lambda a, b: a + b, [total[...] for total in totals])


def first_sum_kernel(subsets, labels, got, out, *totals):
    parts = got.shape[0]
    plane = parts // HALVES
    for total in totals:
        total[...] = jnp.zeros_like(total)

    def one_part(part, carry):
        earlier = jnp.where(part % plane < 4 * subsets, part + plane - 4 * subsets, part - 4 * subsets)
        lister = jnp.where(part // subsets % 4 == 3, earlier, part)
        add_up(labels, [part * PAIRS, lister * PAIRS + 3 * LISTED], got, part, totals)
        return carry

    lax.fori_loop(0, parts, one_part, 0)
    out[...] = together(totals)


def near_sum_kernel(subsets, labels, got, before, out, held, sems, *totals):
    (load,) = fetched([(before, held)], sems)
    for total in totals:
        total[...] = jnp.zeros_like(total)

    def one_part(part, carry):
        lister = part + jnp.where(part // subsets % 2 == 0, subsets, -subsets)
        add_up(labels, [part * PAIRS + LISTED, lister * PAIRS + 2 * LISTED], got, part, totals)
        return carry

    lax.fori_loop(0, got.shape[0], one_part, 0)
    load.wait()
    out[...] = together((held,) + totals).reshape(out.shape).astype(out.dtype)


def body(jacobian, coupling, brick_left, brick_right, tile_target):
    rows = jacobian.shape[1]
    devices = lax.axis_size("tx")
    subsets = lax.axis_size("rep")
    swap, near, far, listing = routes(devices)
    parts = devices * subsets * HALVES
    owners = lax.axis_size("mp_hi") * lax.axis_size("mp_lo")
    slab = BRICK // (parts // HALVES)
    width = BRICK // HALVES
    tiles = owners * TILES_DEV
    smem = pl.BlockSpec(memory_space=pltpu.SMEM)
    vmem = pl.BlockSpec(memory_space=pltpu.VMEM)
    hbm = pl.BlockSpec(memory_space=pl.ANY)
    params = pltpu.CompilerParams(vmem_limit_bytes=24 * 2**20)
    args = [pltpu.with_memory_space_constraint(x, pltpu.HBM) for x in (brick_left, brick_right, tile_target, coupling)]
    whole = pltpu.with_memory_space_constraint(jacobian, pltpu.HBM)
    held = pltpu.VMEM(jacobian.shape[1:], jacobian.dtype)
    copied = pltpu.SemaphoreType.DMA

    near_block = lax.ppermute(jacobian[0], "tx", near)
    far_block = lax.ppermute(jacobian[0], "tx", far)
    place = lax.axis_index("tx") & 3
    spot = place.reshape(1).astype(jnp.int32)

    first = pltpu.HBM((parts, (2 * LISTED + 1) * slab, width), jnp.bfloat16)
    stage = pltpu.VMEM((parts, LISTED * slab, width), jnp.bfloat16)
    meta = jax.ShapeDtypeStruct((1, rows + width), jnp.float32)
    tall = jax.ShapeDtypeStruct((TAIL + 8, jacobian.shape[2]), jnp.float32)
    buffer, own, top, of_one, of_two, of_three = pl.pallas_call(
        own_kernel,
        out_shape=(
            first,
            held,
            pltpu.VMEM((rows - TAIL, jacobian.shape[2]), jacobian.dtype),
            meta,
            tall,
            meta,
        ),
        in_specs=[smem] + [hbm] * 5,
        out_specs=[vmem] * 6,
        scratch_shapes=[
            pltpu.SMEM(brick_left.shape, jnp.int32),
            pltpu.SMEM(brick_right.shape, jnp.int32),
            pltpu.VMEM((2,) + brick_left.shape, jnp.int32),
            pltpu.VMEM(tile_target.shape, jnp.int32),
            pltpu.VMEM(coupling.shape, coupling.dtype),
            pltpu.VMEM((slab, width), jnp.float32),
            copied((10,)),
        ],
        compiler_params=params,
        name="own_products",
    )(spot, *args, whole)
    swapped_top = lax.ppermute(top, "tx", swap)
    of_far = lax.ppermute(of_three, "tx", listing)
    of_swapped = lax.ppermute(of_two, "tx", swap)
    even = place % 2 == 0

    def meta_row(tail):
        return tail[TAIL : TAIL + 1, : rows + width]

    def listed(metas):
        return metas[:, rows : rows + 2 * LISTED].astype(jnp.int32).reshape(-1)

    last = jnp.where(even, of_one, jnp.where(place == 1, of_three, of_far))
    buffer = pl.pallas_call(
        last_kernel,
        out_shape=first,
        in_specs=[smem] + [vmem] * 5 + [hbm],
        out_specs=hbm,
        scratch_shapes=[stage, copied((LISTED // 2,))],
        input_output_aliases={6: 0},
        compiler_params=params,
        name="last_products",
    )(jnp.concatenate([listed(last), spot]), last, own, far_block, swapped_top, of_swapped, buffer)
    got = exchanged(buffer, GROUP)
    labels = got[:, 2 * LISTED * slab, :PAIRS].astype(jnp.int32).reshape(-1)

    metas = jnp.concatenate([jnp.where(even, of_three, of_one), meta_row(of_swapped)], axis=0)
    second = pl.pallas_call(
        near_kernel,
        out_shape=jax.ShapeDtypeStruct((parts, 2 * LISTED * slab, width), jnp.bfloat16),
        in_specs=[smem, vmem, hbm, vmem, vmem, vmem],
        out_specs=vmem,
        scratch_shapes=[held, copied((4,))],
        compiler_params=params,
        cost_estimate=pl.CostEstimate(flops=COST, bytes_accessed=2**23, transcendentals=0),
        name="near_products",
    )(listed(metas), metas, whole, swapped_top, of_swapped, near_block)
    second = exchanged(second, GROUP)

    chains = [pltpu.VMEM((tiles, slab, width), jnp.float32) for _ in range(LISTED)]
    sums = pl.pallas_call(
        functools.partial(first_sum_kernel, subsets),
        out_shape=jax.ShapeDtypeStruct((tiles, slab, width), jnp.float32),
        in_specs=[smem, vmem],
        out_specs=vmem,
        scratch_shapes=chains,
        compiler_params=params,
        name="first_sums",
    )(labels, got)
    sums = pl.pallas_call(
        functools.partial(near_sum_kernel, subsets),
        out_shape=jax.ShapeDtypeStruct((tiles * slab, width), jnp.bfloat16),
        in_specs=[smem, vmem, hbm],
        out_specs=vmem,
        scratch_shapes=[chains[0], copied((1,))] + chains,
        compiler_params=params,
        name="near_sums",
    )(labels, second, pltpu.with_memory_space_constraint(sums, pltpu.HBM))
    sums = exchanged(sums, OWNERS).reshape(owners // HALVES, HALVES, TILES_DEV, slab, width)
    sums = jnp.sum(sums.astype(jnp.float32), axis=0)
    return jnp.concatenate([sums[side] for side in range(HALVES)], axis=-1)


def solution(mesh):
    shape = (mesh.shape["tx"], mesh.shape["mp"] // HALVES, HALVES, mesh.shape["rep"])
    mesh = Mesh(mesh.devices.reshape(shape), ("tx", "mp_hi", "mp_lo", "rep"))
    data = ("mp_hi", "mp_lo", "rep")
    in_specs = (
        P("tx", data, None),
        P(None, "tx", data),
        P("tx", data, None),
        P("tx", data, None),
        P("tx", data, None),
    )
    out_specs = P(OWNERS, ("tx", "rep"), None)
    return jax.shard_map(body, mesh=mesh, in_specs=in_specs, out_specs=out_specs, check_vma=False)
```

```python
import functools

import jax
import jax.numpy as jnp
from jax import lax
from jax.experimental import pallas as pl
from jax.experimental.pallas import tpu as pltpu
from jax.sharding import Mesh, PartitionSpec as P

BRICK = 256
STEPS = 4
LISTED = 6
PAIRS = STEPS * LISTED
TILES_DEV = 8
HALVES = 2
COST = 10**11
TAIL = 16
GROUP = ("mp_lo", "tx", "rep")
OWNERS = ("mp_hi", "mp_lo")


def exchanged(block, axis):
    return lax.all_to_all(block, axis, split_axis=0, concat_axis=0, tiled=True)


def routes(devices):
    everyone = range(devices)
    swap = [(i ^ 1, i) for i in everyone]
    near = [((i + (1 if i % 2 else 3)) % devices, i) for i in everyone]
    far = [((i + (3 if i % 4 == 1 else -4)) % devices, i) for i in everyone if i % 2]
    return swap, near, far, [(source, to) for source, to in far if to % 4 == 3]


def column(row):
    return jnp.broadcast_to(row, (BRICK, row.shape[1])).T


def add_tiles(left_ids, right_ids, weight, left_block, right_block, out, slot, then=None):
    parts = out.shape[0]
    half = parts // HALVES
    slab = BRICK // half
    width = BRICK // HALVES

    def brick(block, index):
        columns = pl.ds(pl.multiple_of(index * BRICK, BRICK), BRICK)
        if not isinstance(block, tuple):
            return block[:, columns]
        top, tail = block
        return jnp.concatenate([top[:, columns], tail[0:TAIL, columns].astype(jnp.bfloat16)], axis=0)

    for first in range(0, LISTED, 2):
        pair = []
        for entry in (first, first + 1):
            left = brick(left_block, left_ids(entry)).astype(jnp.float32) * weight
            tile = lax.dot_general(
                left.astype(jnp.bfloat16),
                brick(right_block, right_ids(entry)),
                (((0,), (0,)), ((), ())),
                preferred_element_type=jnp.float32,
            )
            pair.append(tile.reshape(half, slab, BRICK))
        both = jnp.concatenate(pair, axis=1).astype(jnp.bfloat16)
        row = (slot * LISTED + first) * slab
        for side in range(HALVES):
            out[side * half : (side + 1) * half, row : row + 2 * slab, :] = both[
                :, :, side * width : (side + 1) * width
            ]
        if then is not None:
            then(row, 2 * slab)


def quarters(whole, held):
    rows = held.shape[0] // 4
    return [(whole.at[0, pl.ds(i * rows, rows), :], held.at[pl.ds(i * rows, rows), :]) for i in range(4)]


def fetched(pairs, sems):
    copies = [pltpu.make_async_copy(src, dst, sems.at[i]) for i, (src, dst) in enumerate(pairs)]
    for copy in copies:
        copy.start()
    return copies


def own_kernel(*refs):
    place, left_hbm, right_hbm, targets_hbm, coupling_hbm, whole, out, own, top, *metas = refs[:12]
    left_ids, right_ids, lists, targets, coupling, numbers, sems = refs[12:]
    pairs = (
        (left_hbm, left_ids),
        (right_hbm, right_ids),
        (left_hbm, lists.at[0]),
        (right_hbm, lists.at[1]),
        (targets_hbm, targets),
        (coupling_hbm, coupling),
    ) + tuple(quarters(whole, own))
    copies = fetched(pairs, sems)
    for meta in metas:
        meta[...] = jnp.zeros_like(meta)
    numbers[...] = jnp.zeros_like(numbers)
    for copy in copies[:6]:
        copy.wait()
    even = place[0] % 2 == 0
    for slot, other in enumerate((0, 3, 2, 1)):
        these, those = (targets[0, :, i * LISTED : (i + 1) * LISTED] for i in (slot, other))
        here = slice(slot * LISTED, (slot + 1) * LISTED)
        numbers[0:1, here] = jnp.where(even, those, these).astype(jnp.float32)
    slab = numbers.shape[0]
    below = jnp.broadcast_to(numbers[...].astype(jnp.bfloat16)[None], (out.shape[0],) + numbers.shape)
    out[:, 2 * LISTED * slab :, :] = below
    rows = own.shape[0]
    for step, meta in enumerate(metas, 1):
        here = slice(step * LISTED, (step + 1) * LISTED)
        row = meta.shape[0] // (TAIL + 8) * TAIL
        meta[row : row + 1, 0:rows] = coupling[step]
        for side in range(2):
            first = rows + side * LISTED
            meta[row : row + 1, first : first + LISTED] = lists[side, 0, :, here].astype(jnp.float32)
    for copy in copies[6:]:
        copy.wait()
    top[...] = own[: rows - TAIL, :]
    metas[1][0:TAIL, :] = own[rows - TAIL :, :].astype(jnp.float32)
    add_tiles(lambda i: left_ids[0, 0, i], lambda i: right_ids[0, 0, i], column(coupling[0]), own, own, out, 0)


def pair_of(metas, lists, slot, rows, *blocks_and_out):
    first = slot * 2 * LISTED
    weight = column(metas[slot : slot + 1, 0:rows])
    return (lambda i: lists[first + i], lambda i: lists[first + LISTED + i], weight) + blocks_and_out


def last_kernel(lists, metas, own, *refs):
    far, swapped, (_, out, stage, sems) = refs[0], refs[1:3], refs[3:]
    rows = own.shape[0]
    height = stage.shape[1]
    spot = lists[2 * LISTED]

    def run(left_block, right_block):
        copies = []

        def send(row, size):
            part = stage.at[:, pl.ds(row, size), :]
            copies.append(
                pltpu.make_async_copy(part, out.at[:, pl.ds(height + row, size), :], sems.at[len(copies)])
            )
            copies[-1].start()

        add_tiles(*pair_of(metas, lists, 0, rows, left_block, right_block, stage, 0), send)
        for copy in copies:
            copy.wait()

    pl.when(spot % 2 == 0)(lambda: run(own, swapped))
    pl.when(spot == 1)(lambda: run(own, far))
    pl.when(spot == 3)(lambda: run(far, swapped))


def near_kernel(lists, metas, whole, top, tail, near, out, own, sems):
    swapped = (top, tail)
    loads = fetched(quarters(whole, own), sems)
    rows = own.shape[0]
    add_tiles(*pair_of(metas, lists, 1, rows, swapped, near, out, 1))
    for load in loads:
        load.wait()
    add_tiles(*pair_of(metas, lists, 0, rows, own, near, out, 0))


def add_up(labels, starts, got, part, totals):
    slab = totals[0].shape[1]
    for slot, start in enumerate(starts):
        for first in range(0, LISTED, 2):
            row = (slot * LISTED + first) * slab
            both = got[part, row : row + 2 * slab, :].astype(jnp.float32)
            for side in range(2):
                total = totals[first + side]
                total[labels[start + first + side]] += both[side * slab : (side + 1) * slab]


def together(totals):
    return functools.reduce(lambda a, b: a + b, [total[...] for total in totals])


def first_sum_kernel(subsets, labels, got, out, *totals):
    parts = got.shape[0]
    plane = parts // HALVES
    for total in totals:
        total[...] = jnp.zeros_like(total)

    def one_part(part, carry):
        earlier = jnp.where(part % plane < 4 * subsets, part + plane - 4 * subsets, part - 4 * subsets)
        lister = jnp.where(part // subsets % 4 == 3, earlier, part)
        add_up(labels, [part * PAIRS, lister * PAIRS + 3 * LISTED], got, part, totals)
        return carry

    lax.fori_loop(0, parts, one_part, 0)
    out[...] = together(totals)


def near_sum_kernel(subsets, labels, got, before, out, held, sems, *totals):
    (load,) = fetched([(before, held)], sems)
    for total in totals:
        total[...] = jnp.zeros_like(total)

    def one_part(part, carry):
        lister = part + jnp.where(part // subsets % 2 == 0, subsets, -subsets)
        add_up(labels, [part * PAIRS + LISTED, lister * PAIRS + 2 * LISTED], got, part, totals)
        return carry

    lax.fori_loop(0, got.shape[0], one_part, 0)
    load.wait()
    out[...] = together((held,) + totals).reshape(out.shape).astype(out.dtype)


def body(jacobian, coupling, brick_left, brick_right, tile_target):
    rows = jacobian.shape[1]
    devices = lax.axis_size("tx")
    subsets = lax.axis_size("rep")
    swap, near, far, listing = routes(devices)
    parts = devices * subsets * HALVES
    owners = lax.axis_size("mp_hi") * lax.axis_size("mp_lo")
    slab = BRICK // (parts // HALVES)
    width = BRICK // HALVES
    tiles = owners * TILES_DEV
    smem = pl.BlockSpec(memory_space=pltpu.SMEM)
    vmem = pl.BlockSpec(memory_space=pltpu.VMEM)
    hbm = pl.BlockSpec(memory_space=pl.ANY)
    params = pltpu.CompilerParams(vmem_limit_bytes=24 * 2**20)
    args = [pltpu.with_memory_space_constraint(x, pltpu.HBM) for x in (brick_left, brick_right, tile_target, coupling)]
    whole = pltpu.with_memory_space_constraint(jacobian, pltpu.HBM)
    held = pltpu.VMEM(jacobian.shape[1:], jacobian.dtype)
    copied = pltpu.SemaphoreType.DMA

    near_block = lax.ppermute(jacobian[0], "tx", near)
    far_block = lax.ppermute(jacobian[0], "tx", far)
    place = lax.axis_index("tx") & 3
    spot = place.reshape(1).astype(jnp.int32)

    first = pltpu.HBM((parts, (2 * LISTED + 1) * slab, width), jnp.bfloat16)
    stage = pltpu.VMEM((parts, LISTED * slab, width), jnp.bfloat16)
    meta = jax.ShapeDtypeStruct((1, rows + width), jnp.float32)
    tall = jax.ShapeDtypeStruct((TAIL + 8, jacobian.shape[2]), jnp.float32)
    buffer, own, top, of_one, of_two, of_three = pl.pallas_call(
        own_kernel,
        out_shape=(
            first,
            held,
            pltpu.VMEM((rows - TAIL, jacobian.shape[2]), jacobian.dtype),
            meta,
            tall,
            meta,
        ),
        in_specs=[smem] + [hbm] * 5,
        out_specs=[vmem] * 6,
        scratch_shapes=[
            pltpu.SMEM(brick_left.shape, jnp.int32),
            pltpu.SMEM(brick_right.shape, jnp.int32),
            pltpu.VMEM((2,) + brick_left.shape, jnp.int32),
            pltpu.VMEM(tile_target.shape, jnp.int32),
            pltpu.VMEM(coupling.shape, coupling.dtype),
            pltpu.VMEM((slab, width), jnp.float32),
            copied((10,)),
        ],
        compiler_params=params,
        name="own_products",
    )(spot, *args, whole)
    swapped_top = lax.ppermute(top, "tx", swap)
    of_far = lax.ppermute(of_three, "tx", listing)
    of_swapped = lax.ppermute(of_two, "tx", swap)
    even = place % 2 == 0

    def meta_row(tail):
        return tail[TAIL : TAIL + 1, : rows + width]

    def listed(metas):
        return metas[:, rows : rows + 2 * LISTED].astype(jnp.int32).reshape(-1)

    last = jnp.where(even, of_one, jnp.where(place == 1, of_three, of_far))
    buffer = pl.pallas_call(
        last_kernel,
        out_shape=first,
        in_specs=[smem] + [vmem] * 5 + [hbm],
        out_specs=hbm,
        scratch_shapes=[stage, copied((LISTED // 2,))],
        input_output_aliases={6: 0},
        compiler_params=params,
        name="last_products",
    )(jnp.concatenate([listed(last), spot]), last, own, far_block, swapped_top, of_swapped, buffer)
    got = exchanged(buffer, GROUP)
    labels = got[:, 2 * LISTED * slab, :PAIRS].astype(jnp.int32).reshape(-1)

    metas = jnp.concatenate([jnp.where(even, of_three, of_one), meta_row(of_swapped)], axis=0)
    second = pl.pallas_call(
        near_kernel,
        out_shape=jax.ShapeDtypeStruct((parts, 2 * LISTED * slab, width), jnp.bfloat16),
        in_specs=[smem, vmem, hbm, vmem, vmem, vmem],
        out_specs=vmem,
        scratch_shapes=[held, copied((4,))],
        compiler_params=params,
        cost_estimate=pl.CostEstimate(flops=COST, bytes_accessed=2**23, transcendentals=0),
        name="near_products",
    )(listed(metas), metas, whole, swapped_top, of_swapped, near_block)
    second = exchanged(second, GROUP)

    chains = [pltpu.VMEM((tiles, slab, width), jnp.float32) for _ in range(LISTED)]
    sums = pl.pallas_call(
        functools.partial(first_sum_kernel, subsets),
        out_shape=jax.ShapeDtypeStruct((tiles, slab, width), jnp.float32),
        in_specs=[smem, vmem],
        out_specs=vmem,
        scratch_shapes=chains,
        compiler_params=params,
        name="first_sums",
    )(labels, got)
    sums = pl.pallas_call(
        functools.partial(near_sum_kernel, subsets),
        out_shape=jax.ShapeDtypeStruct((tiles * slab, width), jnp.bfloat16),
        in_specs=[smem, vmem, hbm],
        out_specs=vmem,
        scratch_shapes=[chains[0], copied((1,))] + chains,
        compiler_params=params,
        name="near_sums",
    )(labels, second, pltpu.with_memory_space_constraint(sums, pltpu.HBM))
    sums = exchanged(sums, OWNERS).reshape(owners // HALVES, HALVES, TILES_DEV, slab, width)
    sums = jnp.sum(sums.astype(jnp.float32), axis=0)
    return jnp.concatenate([sums[side] for side in range(HALVES)], axis=-1)


def solution(mesh):
    shape = (mesh.shape["tx"], mesh.shape["mp"] // HALVES, HALVES, mesh.shape["rep"])
    mesh = Mesh(mesh.devices.reshape(shape), ("tx", "mp_hi", "mp_lo", "rep"))
    data = ("mp_hi", "mp_lo", "rep")
    in_specs = (
        P("tx", data, None),
        P(None, "tx", data),
        P("tx", data, None),
        P("tx", data, None),
        P("tx", data, None),
    )
    out_specs = P(OWNERS, ("tx", "rep"), None)
    return jax.shard_map(body, mesh=mesh, in_specs=in_specs, out_specs=out_specs, check_vma=False)
```

```python
import functools

import jax
import jax.numpy as jnp
from jax import lax
from jax.experimental import pallas as pl
from jax.experimental.pallas import tpu as pltpu
from jax.sharding import Mesh, PartitionSpec as P

BRICK = 256
STEPS = 4
LISTED = 6
PAIRS = STEPS * LISTED
TILES_DEV = 8
HALVES = 2
COST = 10**11
TAIL = 16
GROUP = ("mp_lo", "tx", "rep")
OWNERS = ("mp_hi", "mp_lo")


def exchanged(block, axis):
    return lax.all_to_all(block, axis, split_axis=0, concat_axis=0, tiled=True)


def routes(devices):
    everyone = range(devices)
    swap = [(i ^ 1, i) for i in everyone]
    near = [((i + (1 if i % 2 else 3)) % devices, i) for i in everyone]
    far = [((i + (3 if i % 4 == 1 else -4)) % devices, i) for i in everyone if i % 2]
    return swap, near, far, [(source, to) for source, to in far if to % 4 == 3]


def column(row):
    return jnp.broadcast_to(row, (BRICK, row.shape[1])).T


def add_tiles(left_ids, right_ids, weight, left_block, right_block, out, slot, then=None):
    parts = out.shape[0]
    half = parts // HALVES
    slab = BRICK // half
    width = BRICK // HALVES

    def brick(block, index):
        columns = pl.ds(pl.multiple_of(index * BRICK, BRICK), BRICK)
        if not isinstance(block, tuple):
            return block[:, columns]
        top, tail = block
        return jnp.concatenate([top[:, columns], tail[0:TAIL, columns].astype(jnp.bfloat16)], axis=0)

    for first in range(0, LISTED, 2):
        pair = []
        for entry in (first, first + 1):
            left = brick(left_block, left_ids(entry)).astype(jnp.float32) * weight
            tile = lax.dot_general(
                left.astype(jnp.bfloat16),
                brick(right_block, right_ids(entry)),
                (((0,), (0,)), ((), ())),
                preferred_element_type=jnp.float32,
            )
            pair.append(tile.reshape(half, slab, BRICK))
        both = jnp.concatenate(pair, axis=1).astype(jnp.bfloat16)
        row = (slot * LISTED + first) * slab
        for side in range(HALVES):
            out[side * half : (side + 1) * half, row : row + 2 * slab, :] = both[
                :, :, side * width : (side + 1) * width
            ]
        if then is not None:
            then(row, 2 * slab)


def quarters(whole, held):
    rows = held.shape[0] // 4
    return [(whole.at[0, pl.ds(i * rows, rows), :], held.at[pl.ds(i * rows, rows), :]) for i in range(4)]


def fetched(pairs, sems):
    copies = [pltpu.make_async_copy(src, dst, sems.at[i]) for i, (src, dst) in enumerate(pairs)]
    for copy in copies:
        copy.start()
    return copies


def own_kernel(*refs):
    place, left_hbm, right_hbm, targets_hbm, coupling_hbm, whole, out, own, top, *metas = refs[:12]
    left_ids, right_ids, lists, targets, coupling, numbers, sems = refs[12:]
    pairs = (
        (left_hbm, left_ids),
        (right_hbm, right_ids),
        (left_hbm, lists.at[0]),
        (right_hbm, lists.at[1]),
        (targets_hbm, targets),
        (coupling_hbm, coupling),
    ) + tuple(quarters(whole, own))
    copies = fetched(pairs, sems)
    for meta in metas:
        meta[...] = jnp.zeros_like(meta)
    numbers[...] = jnp.zeros_like(numbers)
    for copy in copies[:6]:
        copy.wait()
    even = place[0] % 2 == 0
    for slot, other in enumerate((0, 3, 2, 1)):
        these, those = (targets[0, :, i * LISTED : (i + 1) * LISTED] for i in (slot, other))
        here = slice(slot * LISTED, (slot + 1) * LISTED)
        numbers[0:1, here] = jnp.where(even, those, these).astype(jnp.float32)
    slab = numbers.shape[0]
    below = jnp.broadcast_to(numbers[...].astype(jnp.bfloat16)[None], (out.shape[0],) + numbers.shape)
    out[:, 2 * LISTED * slab :, :] = below
    rows = own.shape[0]
    for step, meta in enumerate(metas, 1):
        here = slice(step * LISTED, (step + 1) * LISTED)
        row = meta.shape[0] // (TAIL + 8) * TAIL
        meta[row : row + 1, 0:rows] = coupling[step]
        for side in range(2):
            first = rows + side * LISTED
            meta[row : row + 1, first : first + LISTED] = lists[side, 0, :, here].astype(jnp.float32)
    for copy in copies[6:]:
        copy.wait()
    top[...] = own[: rows - TAIL, :]
    metas[1][0:TAIL, :] = own[rows - TAIL :, :].astype(jnp.float32)
    add_tiles(lambda i: left_ids[0, 0, i], lambda i: right_ids[0, 0, i], column(coupling[0]), own, own, out, 0)


def pair_of(metas, lists, slot, rows, *blocks_and_out):
    first = slot * 2 * LISTED
    weight = column(metas[slot : slot + 1, 0:rows])
    return (lambda i: lists[first + i], lambda i: lists[first + LISTED + i], weight) + blocks_and_out


def last_kernel(lists, metas, own, *refs):
    far, swapped, (_, out, stage, sems) = refs[0], refs[1:3], refs[3:]
    rows = own.shape[0]
    height = stage.shape[1]
    spot = lists[2 * LISTED]

    def run(left_block, right_block):
        copies = []

        def send(row, size):
            part = stage.at[:, pl.ds(row, size), :]
            copies.append(
                pltpu.make_async_copy(part, out.at[:, pl.ds(height + row, size), :], sems.at[len(copies)])
            )
            copies[-1].start()

        add_tiles(*pair_of(metas, lists, 0, rows, left_block, right_block, stage, 0), send)
        for copy in copies:
            copy.wait()

    pl.when(spot % 2 == 0)(lambda: run(own, swapped))
    pl.when(spot == 1)(lambda: run(own, far))
    pl.when(spot == 3)(lambda: run(far, swapped))


def near_kernel(lists, metas, whole, top, tail, near, out, own, sems):
    swapped = (top, tail)
    loads = fetched(quarters(whole, own), sems)
    rows = own.shape[0]
    add_tiles(*pair_of(metas, lists, 1, rows, swapped, near, out, 1))
    for load in loads:
        load.wait()
    add_tiles(*pair_of(metas, lists, 0, rows, own, near, out, 0))


def add_up(labels, starts, got, part, totals):
    slab = totals[0].shape[1]
    for slot, start in enumerate(starts):
        for first in range(0, LISTED, 2):
            row = (slot * LISTED + first) * slab
            both = got[part, row : row + 2 * slab, :].astype(jnp.float32)
            for side in range(2):
                total = totals[first + side]
                total[labels[start + first + side]] += both[side * slab : (side + 1) * slab]


def together(totals):
    return functools.reduce(lambda a, b: a + b, [total[...] for total in totals])


def first_sum_kernel(subsets, labels, got, out, *totals):
    parts = got.shape[0]
    plane = parts // HALVES
    for total in totals:
        total[...] = jnp.zeros_like(total)

    def one_part(part, carry):
        earlier = jnp.where(part % plane < 4 * subsets, part + plane - 4 * subsets, part - 4 * subsets)
        lister = jnp.where(part // subsets % 4 == 3, earlier, part)
        add_up(labels, [part * PAIRS, lister * PAIRS + 3 * LISTED], got, part, totals)
        return carry

    lax.fori_loop(0, parts, one_part, 0)
    out[...] = together(totals)


def near_sum_kernel(subsets, numbers, got, before, out, labels, held, sems, *totals):
    listing, load = fetched([(numbers, labels), (before, held)], sems)
    for total in totals:
        total[...] = jnp.zeros_like(total)
    listing.wait()

    def one_part(part, carry):
        lister = part + jnp.where(part // subsets % 2 == 0, subsets, -subsets)
        add_up(labels, [part * PAIRS + LISTED, lister * PAIRS + 2 * LISTED], got, part, totals)
        return carry

    lax.fori_loop(0, got.shape[0], one_part, 0, unroll=4)
    load.wait()
    out[...] = together((held,) + totals).reshape(out.shape).astype(out.dtype)


def body(jacobian, coupling, brick_left, brick_right, tile_target):
    rows = jacobian.shape[1]
    devices = lax.axis_size("tx")
    subsets = lax.axis_size("rep")
    swap, near, far, listing = routes(devices)
    parts = devices * subsets * HALVES
    owners = lax.axis_size("mp_hi") * lax.axis_size("mp_lo")
    slab = BRICK // (parts // HALVES)
    width = BRICK // HALVES
    tiles = owners * TILES_DEV
    smem = pl.BlockSpec(memory_space=pltpu.SMEM)
    vmem = pl.BlockSpec(memory_space=pltpu.VMEM)
    hbm = pl.BlockSpec(memory_space=pl.ANY)
    params = pltpu.CompilerParams(vmem_limit_bytes=24 * 2**20)
    args = [pltpu.with_memory_space_constraint(x, pltpu.HBM) for x in (brick_left, brick_right, tile_target, coupling)]
    whole = pltpu.with_memory_space_constraint(jacobian, pltpu.HBM)
    held = pltpu.VMEM(jacobian.shape[1:], jacobian.dtype)
    copied = pltpu.SemaphoreType.DMA

    near_block = lax.ppermute(jacobian[0], "tx", near)
    far_block = lax.ppermute(jacobian[0], "tx", far)
    place = lax.axis_index("tx") & 3
    spot = place.reshape(1).astype(jnp.int32)

    first = pltpu.HBM((parts, (2 * LISTED + 1) * slab, width), jnp.bfloat16)
    stage = pltpu.VMEM((parts, LISTED * slab, width), jnp.bfloat16)
    meta = jax.ShapeDtypeStruct((1, rows + width), jnp.float32)
    tall = jax.ShapeDtypeStruct((TAIL + 8, jacobian.shape[2]), jnp.float32)
    buffer, own, top, of_one, of_two, of_three = pl.pallas_call(
        own_kernel,
        out_shape=(
            first,
            held,
            pltpu.VMEM((rows - TAIL, jacobian.shape[2]), jacobian.dtype),
            meta,
            tall,
            meta,
        ),
        in_specs=[smem] + [hbm] * 5,
        out_specs=[vmem] * 6,
        scratch_shapes=[
            pltpu.SMEM(brick_left.shape, jnp.int32),
            pltpu.SMEM(brick_right.shape, jnp.int32),
            pltpu.VMEM((2,) + brick_left.shape, jnp.int32),
            pltpu.VMEM(tile_target.shape, jnp.int32),
            pltpu.VMEM(coupling.shape, coupling.dtype),
            pltpu.VMEM((slab, width), jnp.float32),
            copied((10,)),
        ],
        compiler_params=params,
        name="own_products",
    )(spot, *args, whole)
    swapped_top = lax.ppermute(top, "tx", swap)
    of_far = lax.ppermute(of_three, "tx", listing)
    of_swapped = lax.ppermute(of_two, "tx", swap)
    even = place % 2 == 0

    def meta_row(tail):
        return tail[TAIL : TAIL + 1, : rows + width]

    def listed(metas):
        return metas[:, rows : rows + 2 * LISTED].astype(jnp.int32).reshape(-1)

    last = jnp.where(even, of_one, jnp.where(place == 1, of_three, of_far))
    buffer = pl.pallas_call(
        last_kernel,
        out_shape=first,
        in_specs=[smem] + [vmem] * 5 + [hbm],
        out_specs=hbm,
        scratch_shapes=[stage, copied((LISTED // 2,))],
        input_output_aliases={6: 0},
        compiler_params=params,
        name="last_products",
    )(jnp.concatenate([listed(last), spot]), last, own, far_block, swapped_top, of_swapped, buffer)
    got = exchanged(buffer, GROUP)
    labels = got[:, 2 * LISTED * slab, :PAIRS].astype(jnp.int32).reshape(-1)

    metas = jnp.concatenate([jnp.where(even, of_three, of_one), meta_row(of_swapped)], axis=0)
    second = pl.pallas_call(
        near_kernel,
        out_shape=jax.ShapeDtypeStruct((parts, 2 * LISTED * slab, width), jnp.bfloat16),
        in_specs=[smem, vmem, hbm, vmem, vmem, vmem],
        out_specs=vmem,
        scratch_shapes=[held, copied((4,))],
        compiler_params=params,
        cost_estimate=pl.CostEstimate(flops=COST, bytes_accessed=2**23, transcendentals=0),
        name="near_products",
    )(listed(metas), metas, whole, swapped_top, of_swapped, near_block)
    second = exchanged(second, GROUP)

    chains = [pltpu.VMEM((tiles, slab, width), jnp.float32) for _ in range(LISTED)]
    sums = pl.pallas_call(
        functools.partial(first_sum_kernel, subsets),
        out_shape=jax.ShapeDtypeStruct((tiles, slab, width), jnp.float32),
        in_specs=[smem, vmem],
        out_specs=vmem,
        scratch_shapes=chains,
        compiler_params=params,
        name="first_sums",
    )(labels, got)
    sums = pl.pallas_call(
        functools.partial(near_sum_kernel, subsets),
        out_shape=jax.ShapeDtypeStruct((tiles * slab, width), jnp.bfloat16),
        in_specs=[hbm, vmem, hbm],
        out_specs=vmem,
        scratch_shapes=[pltpu.SMEM((parts * PAIRS,), jnp.int32), chains[0], copied((2,))] + chains,
        compiler_params=params,
        name="near_sums",
    )(labels, second, pltpu.with_memory_space_constraint(sums, pltpu.HBM))
    sums = exchanged(sums, OWNERS).reshape(owners // HALVES, HALVES, TILES_DEV, slab, width)
    sums = jnp.sum(sums.astype(jnp.float32), axis=0)
    return jnp.concatenate([sums[side] for side in range(HALVES)], axis=-1)


def solution(mesh):
    shape = (mesh.shape["tx"], mesh.shape["mp"] // HALVES, HALVES, mesh.shape["rep"])
    mesh = Mesh(mesh.devices.reshape(shape), ("tx", "mp_hi", "mp_lo", "rep"))
    data = ("mp_hi", "mp_lo", "rep")
    in_specs = (
        P("tx", data, None),
        P(None, "tx", data),
        P("tx", data, None),
        P("tx", data, None),
        P("tx", data, None),
    )
    out_specs = P(OWNERS, ("tx", "rep"), None)
    return jax.shard_map(body, mesh=mesh, in_specs=in_specs, out_specs=out_specs, check_vma=False)
```

```python
import functools

import jax
import jax.numpy as jnp
from jax import lax
from jax.experimental import pallas as pl
from jax.experimental.pallas import tpu as pltpu
from jax.sharding import Mesh, PartitionSpec as P

BRICK = 256
STEPS = 4
LISTED = 6
PAIRS = STEPS * LISTED
TILES_DEV = 8
HALVES = 2
COST = 10**11
TAIL = 16
GROUP = ("mp_lo", "tx", "rep")
OWNERS = ("mp_hi", "mp_lo")


def exchanged(block, axis):
    return lax.all_to_all(block, axis, split_axis=0, concat_axis=0, tiled=True)


def routes(devices):
    everyone = range(devices)
    swap = [(i ^ 1, i) for i in everyone]
    near = [((i + (1 if i % 2 else 3)) % devices, i) for i in everyone]
    far = [((i + (3 if i % 4 == 1 else -4)) % devices, i) for i in everyone if i % 2]
    return swap, near, far, [(source, to) for source, to in far if to % 4 == 3]


def column(row):
    return jnp.broadcast_to(row, (BRICK, row.shape[1])).T


def add_tiles(left_ids, right_ids, weight, left_block, right_block, out, slot, then=None):
    parts = out.shape[0]
    half = parts // HALVES
    slab = BRICK // half
    width = BRICK // HALVES

    def brick(block, index):
        columns = pl.ds(pl.multiple_of(index * BRICK, BRICK), BRICK)
        if not isinstance(block, tuple):
            return block[:, columns]
        top, tail = block
        return jnp.concatenate([top[:, columns], tail[0:TAIL, columns].astype(jnp.bfloat16)], axis=0)

    for first in range(0, LISTED, 2):
        pair = []
        for entry in (first, first + 1):
            left = brick(left_block, left_ids(entry)).astype(jnp.float32) * weight
            tile = lax.dot_general(
                left.astype(jnp.bfloat16),
                brick(right_block, right_ids(entry)),
                (((0,), (0,)), ((), ())),
                preferred_element_type=jnp.float32,
            )
            pair.append(tile.reshape(half, slab, BRICK))
        both = jnp.concatenate(pair, axis=1).astype(jnp.bfloat16)
        row = (slot * LISTED + first) * slab
        for side in range(HALVES):
            out[side * half : (side + 1) * half, row : row + 2 * slab, :] = both[
                :, :, side * width : (side + 1) * width
            ]
        if then is not None:
            then(row, 2 * slab)


def quarters(whole, held):
    rows = held.shape[0] // 4
    return [(whole.at[0, pl.ds(i * rows, rows), :], held.at[pl.ds(i * rows, rows), :]) for i in range(4)]


def fetched(pairs, sems):
    copies = [pltpu.make_async_copy(src, dst, sems.at[i]) for i, (src, dst) in enumerate(pairs)]
    for copy in copies:
        copy.start()
    return copies


def own_kernel(*refs):
    place, left_hbm, right_hbm, targets_hbm, coupling_hbm, whole, out, own, top, *metas = refs[:12]
    left_ids, right_ids, lists, targets, coupling, numbers, sems = refs[12:]
    pairs = (
        (left_hbm, left_ids),
        (right_hbm, right_ids),
        (left_hbm, lists.at[0]),
        (right_hbm, lists.at[1]),
        (targets_hbm, targets),
        (coupling_hbm, coupling),
    ) + tuple(quarters(whole, own))
    copies = fetched(pairs, sems)
    for meta in metas:
        meta[...] = jnp.zeros_like(meta)
    numbers[...] = jnp.zeros_like(numbers)
    for copy in copies[:6]:
        copy.wait()
    even = place[0] % 2 == 0
    for slot, other in enumerate((0, 3, 2, 1)):
        these, those = (targets[0, :, i * LISTED : (i + 1) * LISTED] for i in (slot, other))
        here = slice(slot * LISTED, (slot + 1) * LISTED)
        numbers[0:1, here] = jnp.where(even, those, these).astype(jnp.float32)
    slab = numbers.shape[0]
    below = jnp.broadcast_to(numbers[...].astype(jnp.bfloat16)[None], (out.shape[0],) + numbers.shape)
    out[:, 2 * LISTED * slab :, :] = below
    rows = own.shape[0]
    for step, meta in enumerate(metas, 1):
        here = slice(step * LISTED, (step + 1) * LISTED)
        row = meta.shape[0] // (TAIL + 8) * TAIL
        meta[row : row + 1, 0:rows] = coupling[step]
        for side in range(2):
            first = rows + side * LISTED
            meta[row : row + 1, first : first + LISTED] = lists[side, 0, :, here].astype(jnp.float32)
    for copy in copies[6:]:
        copy.wait()
    top[...] = own[: rows - TAIL, :]
    metas[1][0:TAIL, :] = own[rows - TAIL :, :].astype(jnp.float32)
    add_tiles(lambda i: left_ids[0, 0, i], lambda i: right_ids[0, 0, i], column(coupling[0]), own, own, out, 0)


def pair_of(metas, lists, slot, rows, *blocks_and_out):
    first = slot * 2 * LISTED
    weight = column(metas[slot : slot + 1, 0:rows])
    return (lambda i: lists[first + i], lambda i: lists[first + LISTED + i], weight) + blocks_and_out


def last_kernel(lists, metas, own, *refs):
    far, swapped, (_, out, stage, sems) = refs[0], refs[1:3], refs[3:]
    rows = own.shape[0]
    height = stage.shape[1]
    spot = lists[2 * LISTED]

    def run(left_block, right_block):
        copies = []

        def send(row, size):
            part = stage.at[:, pl.ds(row, size), :]
            copies.append(
                pltpu.make_async_copy(part, out.at[:, pl.ds(height + row, size), :], sems.at[len(copies)])
            )
            copies[-1].start()

        add_tiles(*pair_of(metas, lists, 0, rows, left_block, right_block, stage, 0), send)
        for copy in copies:
            copy.wait()

    pl.when(spot % 2 == 0)(lambda: run(own, swapped))
    pl.when(spot == 1)(lambda: run(own, far))
    pl.when(spot == 3)(lambda: run(far, swapped))


def near_kernel(lists, metas, whole, top, tail, near, out, own, sems):
    swapped = (top, tail)
    loads = fetched(quarters(whole, own), sems)
    rows = own.shape[0]
    add_tiles(*pair_of(metas, lists, 1, rows, swapped, near, out, 1))
    for load in loads:
        load.wait()
    add_tiles(*pair_of(metas, lists, 0, rows, own, near, out, 0))


def add_up(labels, starts, got, part, totals):
    slab = totals[0].shape[1]
    for slot, start in enumerate(starts):
        for first in range(0, LISTED, 2):
            row = (slot * LISTED + first) * slab
            both = got[part, row : row + 2 * slab, :].astype(jnp.float32)
            for side in range(2):
                total = totals[first + side]
                total[labels[start + first + side]] += both[side * slab : (side + 1) * slab]


def together(totals):
    return functools.reduce(lambda a, b: a + b, [total[...] for total in totals])


def first_sum_kernel(subsets, labels, got, out, *totals):
    parts = got.shape[0]
    plane = parts // HALVES
    for total in totals:
        total[...] = jnp.zeros_like(total)

    def one_part(part, carry):
        earlier = jnp.where(part % plane < 4 * subsets, part + plane - 4 * subsets, part - 4 * subsets)
        lister = jnp.where(part // subsets % 4 == 3, earlier, part)
        add_up(labels, [part * PAIRS, lister * PAIRS + 3 * LISTED], got, part, totals)
        return carry

    lax.fori_loop(0, parts, one_part, 0)
    out[...] = together(totals)


def near_sum_kernel(subsets, numbers, got, before, out, labels, held, sems, *totals):
    listing, load = fetched([(numbers, labels), (before, held)], sems)
    for total in totals:
        total[...] = jnp.zeros_like(total)
    listing.wait()

    def one_part(part, carry):
        lister = part + jnp.where(part // subsets % 2 == 0, subsets, -subsets)
        add_up(labels, [part * PAIRS + LISTED, lister * PAIRS + 2 * LISTED], got, part, totals)
        return carry

    lax.fori_loop(0, got.shape[0], one_part, 0, unroll=8)
    load.wait()
    out[...] = together((held,) + totals).reshape(out.shape).astype(out.dtype)


def body(jacobian, coupling, brick_left, brick_right, tile_target):
    rows = jacobian.shape[1]
    devices = lax.axis_size("tx")
    subsets = lax.axis_size("rep")
    swap, near, far, listing = routes(devices)
    parts = devices * subsets * HALVES
    owners = lax.axis_size("mp_hi") * lax.axis_size("mp_lo")
    slab = BRICK // (parts // HALVES)
    width = BRICK // HALVES
    tiles = owners * TILES_DEV
    smem = pl.BlockSpec(memory_space=pltpu.SMEM)
    vmem = pl.BlockSpec(memory_space=pltpu.VMEM)
    hbm = pl.BlockSpec(memory_space=pl.ANY)
    params = pltpu.CompilerParams(vmem_limit_bytes=24 * 2**20)
    args = [pltpu.with_memory_space_constraint(x, pltpu.HBM) for x in (brick_left, brick_right, tile_target, coupling)]
    whole = pltpu.with_memory_space_constraint(jacobian, pltpu.HBM)
    held = pltpu.VMEM(jacobian.shape[1:], jacobian.dtype)
    copied = pltpu.SemaphoreType.DMA

    near_block = lax.ppermute(jacobian[0], "tx", near)
    far_block = lax.ppermute(jacobian[0], "tx", far)
    place = lax.axis_index("tx") & 3
    spot = place.reshape(1).astype(jnp.int32)

    first = pltpu.HBM((parts, (2 * LISTED + 1) * slab, width), jnp.bfloat16)
    stage = pltpu.VMEM((parts, LISTED * slab, width), jnp.bfloat16)
    meta = jax.ShapeDtypeStruct((1, rows + width), jnp.float32)
    tall = jax.ShapeDtypeStruct((TAIL + 8, jacobian.shape[2]), jnp.float32)
    buffer, own, top, of_one, of_two, of_three = pl.pallas_call(
        own_kernel,
        out_shape=(
            first,
            held,
            pltpu.VMEM((rows - TAIL, jacobian.shape[2]), jacobian.dtype),
            meta,
            tall,
            meta,
        ),
        in_specs=[smem] + [hbm] * 5,
        out_specs=[vmem] * 6,
        scratch_shapes=[
            pltpu.SMEM(brick_left.shape, jnp.int32),
            pltpu.SMEM(brick_right.shape, jnp.int32),
            pltpu.VMEM((2,) + brick_left.shape, jnp.int32),
            pltpu.VMEM(tile_target.shape, jnp.int32),
            pltpu.VMEM(coupling.shape, coupling.dtype),
            pltpu.VMEM((slab, width), jnp.float32),
            copied((10,)),
        ],
        compiler_params=params,
        name="own_products",
    )(spot, *args, whole)
    swapped_top = lax.ppermute(top, "tx", swap)
    of_far = lax.ppermute(of_three, "tx", listing)
    of_swapped = lax.ppermute(of_two, "tx", swap)
    even = place % 2 == 0

    def meta_row(tail):
        return tail[TAIL : TAIL + 1, : rows + width]

    def listed(metas):
        return metas[:, rows : rows + 2 * LISTED].astype(jnp.int32).reshape(-1)

    last = jnp.where(even, of_one, jnp.where(place == 1, of_three, of_far))
    buffer = pl.pallas_call(
        last_kernel,
        out_shape=first,
        in_specs=[smem] + [vmem] * 5 + [hbm],
        out_specs=hbm,
        scratch_shapes=[stage, copied((LISTED // 2,))],
        input_output_aliases={6: 0},
        compiler_params=params,
        name="last_products",
    )(jnp.concatenate([listed(last), spot]), last, own, far_block, swapped_top, of_swapped, buffer)
    got = exchanged(buffer, GROUP)
    labels = got[:, 2 * LISTED * slab, :PAIRS].astype(jnp.int32).reshape(-1)

    metas = jnp.concatenate([jnp.where(even, of_three, of_one), meta_row(of_swapped)], axis=0)
    second = pl.pallas_call(
        near_kernel,
        out_shape=jax.ShapeDtypeStruct((parts, 2 * LISTED * slab, width), jnp.bfloat16),
        in_specs=[smem, vmem, hbm, vmem, vmem, vmem],
        out_specs=vmem,
        scratch_shapes=[held, copied((4,))],
        compiler_params=params,
        cost_estimate=pl.CostEstimate(flops=COST, bytes_accessed=2**23, transcendentals=0),
        name="near_products",
    )(listed(metas), metas, whole, swapped_top, of_swapped, near_block)
    second = exchanged(second, GROUP)

    chains = [pltpu.VMEM((tiles, slab, width), jnp.float32) for _ in range(LISTED)]
    sums = pl.pallas_call(
        functools.partial(first_sum_kernel, subsets),
        out_shape=jax.ShapeDtypeStruct((tiles, slab, width), jnp.float32),
        in_specs=[smem, vmem],
        out_specs=vmem,
        scratch_shapes=chains,
        compiler_params=params,
        name="first_sums",
    )(labels, got)
    sums = pl.pallas_call(
        functools.partial(near_sum_kernel, subsets),
        out_shape=jax.ShapeDtypeStruct((tiles * slab, width), jnp.bfloat16),
        in_specs=[hbm, vmem, hbm],
        out_specs=vmem,
        scratch_shapes=[pltpu.SMEM((parts * PAIRS,), jnp.int32), chains[0], copied((2,))] + chains,
        compiler_params=params,
        name="near_sums",
    )(labels, second, pltpu.with_memory_space_constraint(sums, pltpu.HBM))
    sums = exchanged(sums, OWNERS).reshape(owners // HALVES, HALVES, TILES_DEV, slab, width)
    sums = jnp.sum(sums.astype(jnp.float32), axis=0)
    return jnp.concatenate([sums[side] for side in range(HALVES)], axis=-1)


def solution(mesh):
    shape = (mesh.shape["tx"], mesh.shape["mp"] // HALVES, HALVES, mesh.shape["rep"])
    mesh = Mesh(mesh.devices.reshape(shape), ("tx", "mp_hi", "mp_lo", "rep"))
    data = ("mp_hi", "mp_lo", "rep")
    in_specs = (
        P("tx", data, None),
        P(None, "tx", data),
        P("tx", data, None),
        P("tx", data, None),
        P("tx", data, None),
    )
    out_specs = P(OWNERS, ("tx", "rep"), None)
    return jax.shard_map(body, mesh=mesh, in_specs=in_specs, out_specs=out_specs, check_vma=False)
```

```python
import functools

import jax
import jax.numpy as jnp
from jax import lax
from jax.experimental import pallas as pl
from jax.experimental.pallas import tpu as pltpu
from jax.sharding import Mesh, PartitionSpec as P

BRICK = 256
STEPS = 4
LISTED = 6
PAIRS = STEPS * LISTED
TILES_DEV = 8
HALVES = 2
COST = 10**11
TAIL = 16
GROUP = ("mp_lo", "tx", "rep")
OWNERS = ("mp_hi", "mp_lo")


def exchanged(block, axis):
    return lax.all_to_all(block, axis, split_axis=0, concat_axis=0, tiled=True)


def routes(devices):
    everyone = range(devices)
    swap = [(i ^ 1, i) for i in everyone]
    near = [((i + (1 if i % 2 else 3)) % devices, i) for i in everyone]
    far = [((i + (3 if i % 4 == 1 else -4)) % devices, i) for i in everyone if i % 2]
    return swap, near, far, [(source, to) for source, to in far if to % 4 == 3]


def column(row):
    return jnp.broadcast_to(row, (BRICK, row.shape[1])).T


def add_tiles(left_ids, right_ids, weight, left_block, right_block, out, slot, then=None):
    parts = out.shape[0]
    half = parts // HALVES
    slab = BRICK // half
    width = BRICK // HALVES

    def brick(block, index):
        columns = pl.ds(pl.multiple_of(index * BRICK, BRICK), BRICK)
        if not isinstance(block, tuple):
            return block[:, columns]
        top, tail = block
        return jnp.concatenate([top[:, columns], tail[0:TAIL, columns].astype(jnp.bfloat16)], axis=0)

    for first in range(0, LISTED, 2):
        pair = []
        for entry in (first, first + 1):
            left = brick(left_block, left_ids(entry)).astype(jnp.float32) * weight
            tile = lax.dot_general(
                left.astype(jnp.bfloat16),
                brick(right_block, right_ids(entry)),
                (((0,), (0,)), ((), ())),
                preferred_element_type=jnp.float32,
            )
            pair.append(tile.reshape(half, slab, BRICK))
        both = jnp.concatenate(pair, axis=1).astype(jnp.bfloat16)
        row = (slot * LISTED + first) * slab
        for side in range(HALVES):
            out[side * half : (side + 1) * half, row : row + 2 * slab, :] = both[
                :, :, side * width : (side + 1) * width
            ]
        if then is not None:
            then(row, 2 * slab)


def quarters(whole, held):
    rows = held.shape[0] // 4
    return [(whole.at[0, pl.ds(i * rows, rows), :], held.at[pl.ds(i * rows, rows), :]) for i in range(4)]


def fetched(pairs, sems):
    copies = [pltpu.make_async_copy(src, dst, sems.at[i]) for i, (src, dst) in enumerate(pairs)]
    for copy in copies:
        copy.start()
    return copies


def own_kernel(*refs):
    place, left_hbm, right_hbm, targets_hbm, coupling_hbm, whole, out, own, top, *metas = refs[:12]
    left_ids, right_ids, lists, targets, coupling, numbers, sems = refs[12:]
    pairs = (
        (left_hbm, left_ids),
        (right_hbm, right_ids),
        (left_hbm, lists.at[0]),
        (right_hbm, lists.at[1]),
        (targets_hbm, targets),
        (coupling_hbm, coupling),
    ) + tuple(quarters(whole, own))
    copies = fetched(pairs, sems)
    for meta in metas:
        meta[...] = jnp.zeros_like(meta)
    numbers[...] = jnp.zeros_like(numbers)
    for copy in copies[:6]:
        copy.wait()
    even = place[0] % 2 == 0
    for slot, other in enumerate((0, 3, 2, 1)):
        these, those = (targets[0, :, i * LISTED : (i + 1) * LISTED] for i in (slot, other))
        here = slice(slot * LISTED, (slot + 1) * LISTED)
        numbers[0:1, here] = jnp.where(even, those, these).astype(jnp.float32)
    slab = numbers.shape[0]
    below = jnp.broadcast_to(numbers[...].astype(jnp.bfloat16)[None], (out.shape[0],) + numbers.shape)
    out[:, 2 * LISTED * slab :, :] = below
    rows = own.shape[0]
    for step, meta in enumerate(metas, 1):
        here = slice(step * LISTED, (step + 1) * LISTED)
        row = meta.shape[0] // (TAIL + 8) * TAIL
        meta[row : row + 1, 0:rows] = coupling[step]
        for side in range(2):
            first = rows + side * LISTED
            meta[row : row + 1, first : first + LISTED] = lists[side, 0, :, here].astype(jnp.float32)
    for copy in copies[6:]:
        copy.wait()
    top[...] = own[: rows - TAIL, :]
    metas[1][0:TAIL, :] = own[rows - TAIL :, :].astype(jnp.float32)
    add_tiles(lambda i: left_ids[0, 0, i], lambda i: right_ids[0, 0, i], column(coupling[0]), own, own, out, 0)


def pair_of(metas, lists, slot, rows, *blocks_and_out):
    first = slot * 2 * LISTED
    weight = column(metas[slot : slot + 1, 0:rows])
    return (lambda i: lists[first + i], lambda i: lists[first + LISTED + i], weight) + blocks_and_out


def last_kernel(lists, metas, own, *refs):
    far, swapped, (_, out, stage, sems) = refs[0], refs[1:3], refs[3:]
    rows = own.shape[0]
    height = stage.shape[1]
    spot = lists[2 * LISTED]

    def run(left_block, right_block):
        copies = []

        def send(row, size):
            part = stage.at[:, pl.ds(row, size), :]
            copies.append(
                pltpu.make_async_copy(part, out.at[:, pl.ds(height + row, size), :], sems.at[len(copies)])
            )
            copies[-1].start()

        add_tiles(*pair_of(metas, lists, 0, rows, left_block, right_block, stage, 0), send)
        for copy in copies:
            copy.wait()

    pl.when(spot % 2 == 0)(lambda: run(own, swapped))
    pl.when(spot == 1)(lambda: run(own, far))
    pl.when(spot == 3)(lambda: run(far, swapped))


def near_kernel(lists, metas, whole, top, tail, near, out, own, sems):
    swapped = (top, tail)
    loads = fetched(quarters(whole, own), sems)
    rows = own.shape[0]
    add_tiles(*pair_of(metas, lists, 1, rows, swapped, near, out, 1))
    for load in loads:
        load.wait()
    add_tiles(*pair_of(metas, lists, 0, rows, own, near, out, 0))


def add_up(labels, starts, got, part, totals):
    slab = totals[0].shape[1]
    for slot, start in enumerate(starts):
        for first in range(0, LISTED, 2):
            row = (slot * LISTED + first) * slab
            both = got[part, row : row + 2 * slab, :].astype(jnp.float32)
            for side in range(2):
                total = totals[first + side]
                total[labels[start + first + side]] += both[side * slab : (side + 1) * slab]


def together(totals):
    return functools.reduce(lambda a, b: a + b, [total[...] for total in totals])


def first_sum_kernel(subsets, labels, got, out, *totals):
    parts = got.shape[0]
    plane = parts // HALVES
    for total in totals:
        total[...] = jnp.zeros_like(total)

    def one_part(part, carry):
        earlier = jnp.where(part % plane < 4 * subsets, part + plane - 4 * subsets, part - 4 * subsets)
        lister = jnp.where(part // subsets % 4 == 3, earlier, part)
        add_up(labels, [part * PAIRS, lister * PAIRS + 3 * LISTED], got, part, totals)
        return carry

    lax.fori_loop(0, parts, one_part, 0)
    out[...] = together(totals)


def near_sum_kernel(subsets, numbers, got, before, out, labels, held, sems, *totals):
    listing, load = fetched([(numbers, labels), (before, held)], sems)
    for total in totals:
        total[...] = jnp.zeros_like(total)
    listing.wait()

    def one_part(part, carry):
        lister = part + jnp.where(part // subsets % 2 == 0, subsets, -subsets)
        add_up(labels, [part * PAIRS + LISTED, lister * PAIRS + 2 * LISTED], got, part, totals)
        return carry

    lax.fori_loop(0, got.shape[0], one_part, 0, unroll=16)
    load.wait()
    out[...] = together((held,) + totals).reshape(out.shape).astype(out.dtype)


def body(jacobian, coupling, brick_left, brick_right, tile_target):
    rows = jacobian.shape[1]
    devices = lax.axis_size("tx")
    subsets = lax.axis_size("rep")
    swap, near, far, listing = routes(devices)
    parts = devices * subsets * HALVES
    owners = lax.axis_size("mp_hi") * lax.axis_size("mp_lo")
    slab = BRICK // (parts // HALVES)
    width = BRICK // HALVES
    tiles = owners * TILES_DEV
    smem = pl.BlockSpec(memory_space=pltpu.SMEM)
    vmem = pl.BlockSpec(memory_space=pltpu.VMEM)
    hbm = pl.BlockSpec(memory_space=pl.ANY)
    params = pltpu.CompilerParams(vmem_limit_bytes=24 * 2**20)
    args = [pltpu.with_memory_space_constraint(x, pltpu.HBM) for x in (brick_left, brick_right, tile_target, coupling)]
    whole = pltpu.with_memory_space_constraint(jacobian, pltpu.HBM)
    held = pltpu.VMEM(jacobian.shape[1:], jacobian.dtype)
    copied = pltpu.SemaphoreType.DMA

    near_block = lax.ppermute(jacobian[0], "tx", near)
    far_block = lax.ppermute(jacobian[0], "tx", far)
    place = lax.axis_index("tx") & 3
    spot = place.reshape(1).astype(jnp.int32)

    first = pltpu.HBM((parts, (2 * LISTED + 1) * slab, width), jnp.bfloat16)
    stage = pltpu.VMEM((parts, LISTED * slab, width), jnp.bfloat16)
    meta = jax.ShapeDtypeStruct((1, rows + width), jnp.float32)
    tall = jax.ShapeDtypeStruct((TAIL + 8, jacobian.shape[2]), jnp.float32)
    buffer, own, top, of_one, of_two, of_three = pl.pallas_call(
        own_kernel,
        out_shape=(
            first,
            held,
            pltpu.VMEM((rows - TAIL, jacobian.shape[2]), jacobian.dtype),
            meta,
            tall,
            meta,
        ),
        in_specs=[smem] + [hbm] * 5,
        out_specs=[vmem] * 6,
        scratch_shapes=[
            pltpu.SMEM(brick_left.shape, jnp.int32),
            pltpu.SMEM(brick_right.shape, jnp.int32),
            pltpu.VMEM((2,) + brick_left.shape, jnp.int32),
            pltpu.VMEM(tile_target.shape, jnp.int32),
            pltpu.VMEM(coupling.shape, coupling.dtype),
            pltpu.VMEM((slab, width), jnp.float32),
            copied((10,)),
        ],
        compiler_params=params,
        name="own_products",
    )(spot, *args, whole)
    swapped_top = lax.ppermute(top, "tx", swap)
    of_far = lax.ppermute(of_three, "tx", listing)
    of_swapped = lax.ppermute(of_two, "tx", swap)
    even = place % 2 == 0

    def meta_row(tail):
        return tail[TAIL : TAIL + 1, : rows + width]

    def listed(metas):
        return metas[:, rows : rows + 2 * LISTED].astype(jnp.int32).reshape(-1)

    last = jnp.where(even, of_one, jnp.where(place == 1, of_three, of_far))
    buffer = pl.pallas_call(
        last_kernel,
        out_shape=first,
        in_specs=[smem] + [vmem] * 5 + [hbm],
        out_specs=hbm,
        scratch_shapes=[stage, copied((LISTED // 2,))],
        input_output_aliases={6: 0},
        compiler_params=params,
        name="last_products",
    )(jnp.concatenate([listed(last), spot]), last, own, far_block, swapped_top, of_swapped, buffer)
    got = exchanged(buffer, GROUP)
    labels = got[:, 2 * LISTED * slab, :PAIRS].astype(jnp.int32).reshape(-1)

    metas = jnp.concatenate([jnp.where(even, of_three, of_one), meta_row(of_swapped)], axis=0)
    second = pl.pallas_call(
        near_kernel,
        out_shape=jax.ShapeDtypeStruct((parts, 2 * LISTED * slab, width), jnp.bfloat16),
        in_specs=[smem, vmem, hbm, vmem, vmem, vmem],
        out_specs=vmem,
        scratch_shapes=[held, copied((4,))],
        compiler_params=params,
        cost_estimate=pl.CostEstimate(flops=COST, bytes_accessed=2**23, transcendentals=0),
        name="near_products",
    )(listed(metas), metas, whole, swapped_top, of_swapped, near_block)
    second = exchanged(second, GROUP)

    chains = [pltpu.VMEM((tiles, slab, width), jnp.float32) for _ in range(LISTED)]
    sums = pl.pallas_call(
        functools.partial(first_sum_kernel, subsets),
        out_shape=jax.ShapeDtypeStruct((tiles, slab, width), jnp.float32),
        in_specs=[smem, vmem],
        out_specs=vmem,
        scratch_shapes=chains,
        compiler_params=params,
        name="first_sums",
    )(labels, got)
    sums = pl.pallas_call(
        functools.partial(near_sum_kernel, subsets),
        out_shape=jax.ShapeDtypeStruct((tiles * slab, width), jnp.bfloat16),
        in_specs=[hbm, vmem, hbm],
        out_specs=vmem,
        scratch_shapes=[pltpu.SMEM((parts * PAIRS,), jnp.int32), chains[0], copied((2,))] + chains,
        compiler_params=params,
        name="near_sums",
    )(labels, second, pltpu.with_memory_space_constraint(sums, pltpu.HBM))
    sums = exchanged(sums, OWNERS).reshape(owners // HALVES, HALVES, TILES_DEV, slab, width)
    sums = jnp.sum(sums.astype(jnp.float32), axis=0)
    return jnp.concatenate([sums[side] for side in range(HALVES)], axis=-1)


def solution(mesh):
    shape = (mesh.shape["tx"], mesh.shape["mp"] // HALVES, HALVES, mesh.shape["rep"])
    mesh = Mesh(mesh.devices.reshape(shape), ("tx", "mp_hi", "mp_lo", "rep"))
    data = ("mp_hi", "mp_lo", "rep")
    in_specs = (
        P("tx", data, None),
        P(None, "tx", data),
        P("tx", data, None),
        P("tx", data, None),
        P("tx", data, None),
    )
    out_specs = P(OWNERS, ("tx", "rep"), None)
    return jax.shard_map(body, mesh=mesh, in_specs=in_specs, out_specs=out_specs, check_vma=False)
```
